256 devices in a mesh: section: 8 (over z), cp: 32 (over y, x, core).
Axes of the slice: x: 4, y: 4, z: 8, core: 2. Of those that a mesh axis runs over, the one named last changes fastest.
Arguments:
- inputs: bfloat16 [2, 5120, 2048], P(None, 'cp'), may hold values from -6 to 6
- norm_gain: float32 [8, 2048], P('section'), may hold values from 0.1 to 1.9
- qkv_weight: bfloat16 [8, 2048, 3072], P('section', 'cp')
- batch_lengths: int32 [2], replicated, may hold values from 2560 to 5120, as said below
- doc_lengths: int32 [2, 128], replicated, may hold values from 1 to 160, 5120 in all within a row
- doc_shift: int32 [2, 128], replicated, may hold values 0 or 1
Outputs:
- section_out: bfloat16 [8, 2, 10240, 2048], P('section', None, 'cp')
The draws below stay inside these ranges and needn't reach their ends.
Inputs may be any that keep to these rules, and one draw needn't show every extreme that they name: `batch_lengths`: one micro-batch in every draw holds all 5120 rows. `doc_lengths`: the lengths of a micro-batch sum to 5120.
All inputs are finite; a program needn't handle non-finite values.
Results may differ from the reference program's by a relative error of at most 0.015.
Values may be sent and summed in bfloat16 or wider, within the bound.
A program may use at most 64 MiB of HBM per device.

```python
import math
import jax
import jax.numpy as jnp
import numpy as np
from jax import lax

D = 2048
QHEADS = 16
KVHEADS = 4
HEAD_DIM = 128
ROWS = 160
MICRO = 2
LAYERS = 8
MB_ROWS = 5120
NDOCS = 128
N_CP = 32


def draw_qkv_weight(key, part):
    key = jax.random.fold_in(key, 7)
    columns = (QHEADS + 2 * KVHEADS) * HEAD_DIM
    drawn = jnp.clip(jax.random.normal(key, (LAYERS, D, columns), jnp.float32), -6.0, 6.0) / math.sqrt(D)
    return drawn.astype(jnp.bfloat16)


def draw_batch_lengths(key, part):
    key = jax.random.fold_in(key, 11)
    spread_key, pick_key = jax.random.split(key)
    lengths = jax.random.randint(spread_key, (MICRO,), MB_ROWS // 2, MB_ROWS + 1)
    chosen = jax.random.randint(pick_key, (), 0, MICRO)
    return jnp.where(jnp.arange(MICRO) == chosen, MB_ROWS, lengths).astype(jnp.int32)


def with_ends(result, stream_key, low, top_value):
    spot = [jax.random.randint(jax.random.fold_in(stream_key, axis), (), 0, length) for axis, length in enumerate(result.shape)]
    widest = result.shape.index(max(result.shape))
    next_to = spot[:widest] + [(spot[widest] + 1) % result.shape[widest]] + spot[widest + 1:]
    return result.at[tuple(spot)].set(low).at[tuple(next_to)].set(top_value)


def block_levels(rng, shape, cuts, least, high):
    level = 1.0
    for position, shards_of in cuts:
        steps = jax.random.uniform(jax.random.fold_in(jax.random.fold_in(rng, 6), position), (shards_of,), jnp.float32, least / len(cuts), high / len(cuts))
        level = level * jnp.repeat(jnp.exp(steps), shape[position] // shards_of).reshape((-1,) + (1,) * (len(shape) - 1 - position))
    return level


def split_up(amount, total, most, lean):
    portions = [(1 << 20) // math.isqrt(grade ** lean) + 1 for grade in range(2, amount + 1)]
    rest, given = total - most - (amount - 1), [1] * (amount - 1)
    while rest > 0:
        free = [i for i in range(amount - 1) if given[i] < most]
        whole, left = sum([portions[i] for i in free]), rest
        for i in free:
            addition = min(most - given[i], max(1, left * portions[i] // whole), rest)
            given[i] = given[i] + addition
            rest = rest - addition
    return np.array([most] + given)


def uneven(rng, amount, total, reach, slope):
    if amount == 2:
        one = jax.random.randint(rng, (), max(1, total - reach), min(reach, total - 1) + 1)
        return jnp.stack([one, total - one])
    tallies = jnp.asarray(split_up(amount, total, reach, slope), jnp.int32)
    couples = (amount - 1) // 2
    donor, receiver = tallies[1:1 + 2 * couples:2], tallies[2:2 + 2 * couples:2]
    slack = jnp.minimum(donor - 1, reach - receiver)
    moved = jax.random.randint(jax.random.fold_in(rng, 1), (couples,), 0, 1 << 20) % (slack + 1)
    tallies = tallies.at[1:1 + 2 * couples:2].set(donor - moved).at[2:2 + 2 * couples:2].set(receiver + moved)
    return tallies[jax.random.permutation(jax.random.fold_in(rng, 2), amount)]


def gaussian(rng, extent, width, limit, cuts=(), held_as=jnp.bfloat16):
    values = jax.random.normal(rng, extent, jnp.float32) * width
    if len(cuts) > 0:
        values = block_levels(rng, extent, cuts, -0.22, 0.18) * values
    return jnp.clip(values, min=-limit, max=limit).astype(held_as)


def setup_inputs(seed: int = 0) -> dict:
    key_of = jax.random.split(jax.random.key(seed), 7)
    inputs = gaussian(key_of[0], (MICRO, MB_ROWS, D), 1.0, 6.0, ((1, 32),))
    norm_gain = jnp.clip(1.0 + 0.18 * jax.random.normal(key_of[1], (LAYERS, D), jnp.float32), 0.1, 1.9)
    qkv_weight = draw_qkv_weight(jax.random.fold_in(key_of[6], 71), 0)
    batch_lengths = draw_batch_lengths(jax.random.fold_in(key_of[6], 71), 0)
    doc_lengths = jax.vmap(lambda own: uneven(own, NDOCS, MB_ROWS, ROWS, 2))(jax.random.split(key_of[4], MICRO)).reshape((MICRO, NDOCS)).astype(jnp.int32)
    doc_shift = with_ends((jax.random.randint(key_of[5], (MICRO, NDOCS), 0, 2) < 1).astype(jnp.int32), jax.random.fold_in(key_of[5], 1), 0, 1)
    return {"inputs": inputs, "norm_gain": norm_gain, "qkv_weight": qkv_weight, "batch_lengths": batch_lengths, "doc_lengths": doc_lengths, "doc_shift": doc_shift}


EPSILON = 1e-05
NEGATIVE = -1e+30

def project(state, gains, weights):
    values = state.astype(jnp.float32)
    inverse = lax.rsqrt(lax.optimization_barrier(jnp.mean(values * values, axis=1, keepdims=True)) + EPSILON)
    normed = (values * inverse * gains[None, :]).astype(jnp.bfloat16)
    projected = jnp.dot(normed, weights, preferred_element_type=jnp.float32).astype(jnp.bfloat16)
    return lax.optimization_barrier(projected)

def split_heads(projected, model_width, kv_heads, head_size):
    row_count = projected.shape[0]
    group_size = model_width // head_size // kv_heads
    queries = projected[:, :model_width].reshape(row_count, kv_heads, group_size, head_size)
    key_rows = projected[:, model_width:model_width + kv_heads * head_size].reshape(row_count, kv_heads, head_size)
    val_rows = projected[:, model_width + kv_heads * head_size:].reshape(row_count, kv_heads, head_size)
    return (queries, key_rows, val_rows)

def mix(queries, key_rows, val_rows, query_docs, key_docs, query_places, key_places, key_living):
    head_size = queries.shape[3]
    scores = jnp.einsum('ikgd,jkd->kgij', queries.astype(jnp.float32), key_rows.astype(jnp.float32)) / math.sqrt(head_size)
    same_place = key_places[None, :] == query_places[:, None]
    allowed = (query_docs[:, None] == key_docs[None, :]) & (key_places[None, :] <= query_places[:, None]) & (key_living[None, :] | same_place)
    scores = jnp.where(allowed, scores, NEGATIVE)
    highest = lax.optimization_barrier(jnp.max(scores, axis=3, keepdims=True))
    weighted = jnp.where(allowed, jnp.exp(scores - highest), 0.0)
    totals = lax.optimization_barrier(jnp.sum(weighted, axis=3, keepdims=True))
    shares = lax.optimization_barrier((weighted / totals).astype(jnp.bfloat16)).astype(jnp.float32)
    mixture = jnp.einsum('kgij,jkd->ikgd', shares, val_rows.astype(jnp.float32))
    return mixture.reshape(queries.shape[0], -1)

def row_layout(batch_length, lengths, shifts):
    places = jnp.arange(MB_ROWS, dtype=jnp.int32)
    ends = jnp.cumsum(lengths).astype(jnp.int32)
    starts = (ends - lengths).astype(jnp.int32)
    first_rank = starts // ROWS
    last_rank = (ends - 1) // ROWS
    movable = ((first_rank == last_rank) & (last_rank < N_CP - 1)).astype(jnp.int32)
    target_doc = (last_rank + shifts * movable).astype(jnp.int32)
    doc_ids = lax.optimization_barrier(jnp.sum((starts[None, :] <= places[:, None]).astype(jnp.int32), axis=1)).astype(jnp.int32) - 1
    matches = doc_ids[:, None] == jnp.arange(NDOCS, dtype=jnp.int32)[None, :]
    targets = lax.optimization_barrier(jnp.sum(jnp.where(matches, target_doc[None, :], 0), axis=1)).astype(jnp.int32)
    living = places < batch_length
    return (places, doc_ids, targets, living)

def windows(array):
    tail = array.shape[1:]
    return jnp.concatenate([array[:MB_ROWS].reshape((N_CP, ROWS) + tail), array[ROWS:].reshape((N_CP, ROWS) + tail)], axis=1)

def apply_layer(state, places, doc_ids, living, gains, weights):
    model_width = state.shape[1]
    projected = project(state, gains, weights)
    pad_proj = jnp.concatenate([jnp.zeros((ROWS, projected.shape[1]), projected.dtype), projected])
    pad_docs = jnp.concatenate([jnp.full((ROWS,), -2, jnp.int32), doc_ids])
    pad_places = jnp.concatenate([jnp.arange(ROWS, dtype=jnp.int32) - ROWS, places])
    pad_living = jnp.concatenate([jnp.zeros((ROWS,), jnp.bool_), living])

    def one_block(pieces):
        block_proj, block_docs, block_places, block_living = pieces
        queries, key_rows, val_rows = split_heads(block_proj, model_width, KVHEADS, HEAD_DIM)
        return mix(queries[ROWS:], key_rows, val_rows, block_docs[ROWS:], block_docs, block_places[ROWS:], block_places, block_living)
    mixture = lax.map(one_block, (windows(pad_proj), windows(pad_docs), windows(pad_places), windows(pad_living)))
    mixture = mixture.reshape(MB_ROWS, model_width)
    return jnp.where(living[:, None], state.astype(jnp.float32) + mixture, 0.0).astype(jnp.bfloat16)

def route_rows(state, targets, living):
    model_width = state.shape[1]
    own_target = jnp.where(living, targets, -1).astype(jnp.int32)
    padded_state = jnp.concatenate([jnp.zeros((ROWS, model_width), state.dtype), state])
    padded_target = jnp.concatenate([jnp.full((ROWS,), -1, jnp.int32), own_target])
    left_rows = padded_state[:MB_ROWS].reshape(N_CP, ROWS, model_width)
    own_rows = state.reshape(N_CP, ROWS, model_width)
    left_target = padded_target[:MB_ROWS].reshape(N_CP, ROWS)
    owner = jnp.arange(N_CP, dtype=jnp.int32)[:, None]
    routed = jnp.concatenate([jnp.where((left_target == owner)[:, :, None], left_rows, 0), jnp.where((own_target.reshape(N_CP, ROWS) == owner)[:, :, None], own_rows, 0)], axis=1)
    return routed.reshape(2 * MB_ROWS, model_width)

def reference(inputs, norm_gain, qkv_weight, batch_lengths, doc_lengths, doc_shift):
    results = []
    for batch_index in range(MICRO):
        places, doc_ids, targets, living = row_layout(batch_lengths[batch_index], doc_lengths[batch_index], doc_shift[batch_index])
        state = jnp.where(living[:, None], inputs[batch_index], 0).astype(jnp.bfloat16)
        layers_out = []
        for layer_index in range(LAYERS):
            state = apply_layer(state, places, doc_ids, living, norm_gain[layer_index], qkv_weight[layer_index])
            layers_out.append(route_rows(state, targets, living))
        results.append(jnp.stack(layers_out))
    return jnp.stack(results, axis=1)
```

```python
import functools
import math

import jax
import jax.numpy as jnp
from jax import lax
from jax.experimental import pallas as pl
from jax.experimental.pallas import tpu as pltpu
from jax.sharding import PartitionSpec as P

MESH = pl.DeviceIdType.MESH
KVHEADS = 4
HEAD = 128
GROUP = 4
WIDE = GROUP * HEAD
COLS = WIDE + 2 * HEAD
NX, NY = 4, 4
EPSILON = 1e-05
NEGATIVE = -1e30
BF, F32 = jnp.bfloat16, jnp.float32


def kernel(
    inp, gain, w, lens, shifts, blen, out,
    wv, xin, xn, new, keep, pass_on, kv, halo, qs, allow, live, sel_a, sel_b,
    s1s, s1r, s2s, s2r, s3s, s3r, s4s, s4r, ds, dr,
    hs, hr, zs, zr, as_, bs, br,
):
    z, r = lax.axis_index("section"), lax.axis_index("cp")
    last_z = lax.axis_size("section") - 1
    ranks = lax.axis_size("cp")
    c = r % 2
    x, y = (r // 2) % NX, r // (2 * NX)
    chunks, groups, rows = xin.shape[0], xin.shape[1], xin.shape[2]
    width = groups * WIDE
    back = halo.shape[3]

    def at(dx, dy):
        return (z, (((y + dy) % NY) * NX + (x + dx) % NX) * 2 + c)

    sibling = (z, r + 1 - 2 * c)
    right, left = (z, (r + 1) % ranks), (z, (r + ranks - 1) % ranks)
    above = ((z + 1) % (last_z + 1), r)
    below = ((z + last_z) % (last_z + 1), r)

    barrier = pltpu.get_barrier_semaphore()
    peers = [sibling, at(1, 0), at(3, 0), at(0, 1), at(0, 3), right, left, above, below]
    for peer in peers:
        pl.semaphore_signal(barrier, inc=1, device_id=peer, device_id_type=MESH)

    for g in range(groups):
        for f in range(2):
            part = pl.ds(32 * f, 32)
            wv[g, y, x, c, f, :, 0:WIDE] = w[0, part, g * WIDE : (g + 1) * WIDE]
            for k in range(2):
                first = width + (k * groups + g) * HEAD
                wv[g, y, x, c, f, :, WIDE + k * HEAD : WIDE + (k + 1) * HEAD] = w[
                    0, part, first : first + HEAD
                ]
    pl.semaphore_wait(barrier, len(peers))

    def send(src, dst, ss, rs, to):
        return pltpu.make_async_remote_copy(
            src_ref=src, dst_ref=dst, send_sem=ss, recv_sem=rs, device_id=to, device_id_type=MESH
        )

    def same(ref, ss, rs, to):
        return send(ref, ref, ss, rs, to)

    x1, x3, y1, y3 = (x + 1) % NX, (x + 3) % NX, (y + 1) % NY, (y + 3) % NY
    x2, y2 = (x + 2) % NX, (y + 2) % NY
    low, high = pl.ds(0, 16), pl.ds(16, 16)

    def step1(g):
        return [
            same(wv.at[g, y, x, c, 0], s1s.at[0, g, 0], s1r.at[0, g, 0], at(1, 0)),
            same(wv.at[g, y, x, c, 0], s1s.at[0, g, 1], s1r.at[0, g, 1], at(3, 0)),
            same(wv.at[g, y, x, c, 1], s1s.at[1, g, 0], s1r.at[1, g, 0], at(0, 1)),
            same(wv.at[g, y, x, c, 1], s1s.at[1, g, 1], s1r.at[1, g, 1], at(0, 3)),
        ]

    def step2(g):
        return [
            same(wv.at[g, y, x3, c, 0, low], s2s.at[0, g, 0], s2r.at[0, g, 0], at(1, 0)),
            same(wv.at[g, y, x1, c, 0, high], s2s.at[0, g, 1], s2r.at[0, g, 1], at(3, 0)),
            same(wv.at[g, y3, x, c, 1, low], s2s.at[1, g, 0], s2r.at[1, g, 0], at(0, 1)),
            same(wv.at[g, y1, x, c, 1, high], s2s.at[1, g, 1], s2r.at[1, g, 1], at(0, 3)),
        ]

    def step3(g):
        return [
            same(wv.at[g, y, :, c, 0], s3s.at[0, g, 0], s3r.at[0, g, 0], at(0, 1)),
            same(wv.at[g, y, :, c, 0], s3s.at[0, g, 1], s3r.at[0, g, 1], at(0, 3)),
            same(wv.at[g, :, x, c, 1], s3s.at[1, g, 0], s3r.at[1, g, 0], at(1, 0)),
            same(wv.at[g, :, x, c, 1], s3s.at[1, g, 1], s3r.at[1, g, 1], at(3, 0)),
        ]

    def step4(g):
        return [
            same(wv.at[g, y3, :, c, 0, low], s4s.at[0, g, 0], s4r.at[0, g, 0], at(0, 1)),
            same(wv.at[g, y1, :, c, 0, high], s4s.at[0, g, 1], s4r.at[0, g, 1], at(0, 3)),
            same(wv.at[g, :, x3, c, 1, low], s4s.at[1, g, 0], s4r.at[1, g, 0], at(1, 0)),
            same(wv.at[g, :, x1, c, 1, high], s4s.at[1, g, 1], s4r.at[1, g, 1], at(3, 0)),
        ]

    def share(g, which):
        row, col = ((y, x), (y3, x3), (y1, x1), (y2, x2))[which]
        return [
            same(wv.at[g, row, :, c, 0], ds.at[0, g, which], dr.at[0, g, which], sibling),
            same(wv.at[g, :, col, c, 1], ds.at[1, g, which], dr.at[1, g, which], sibling),
        ]

    def start(copies):
        for copy in copies:
            copy.start()

    def arrive(copies):
        for copy in copies:
            copy.wait_recv()

    def sent(copies):
        for copy in copies:
            copy.wait_send()

    @pl.loop(0, groups)
    def _(g):
        start(step1(g))

    spot = lax.broadcasted_iota(jnp.int32, (HEAD, HEAD), 0)
    until = lax.broadcasted_iota(jnp.int32, (HEAD, HEAD), 1)
    upto = jnp.where(spot <= until, 1.0, 0.0).astype(BF)
    length = lens[...].astype(F32)
    ends = jnp.dot(length.astype(BF), upto, preferred_element_type=F32)
    starts = ends - length
    moves = shifts[...].astype(F32)
    base = (r * rows).astype(F32)
    for q in range(chunks):
        begin, end, move = starts[q : q + 1], ends[q : q + 1], moves[q : q + 1]
        place = lax.broadcasted_iota(jnp.int32, (rows, HEAD), 0).astype(F32) + base
        before, after = begin <= place, end > place
        doc_start = jnp.max(jnp.where(before, begin, -1.0), axis=1, keepdims=True)
        doc_end = jnp.min(jnp.where(after, end, 1e9), axis=1, keepdims=True)
        shift = jnp.max(jnp.where(before & after, move, 0.0), axis=1, keepdims=True)
        edge = base + rows
        moved = (doc_start >= base) & (shift > 0.5) & (edge < float(rows) * ranks)
        to_next = jnp.where((doc_end > edge) | moved, 1.0, 0.0)
        alive = jnp.where(place < blen[q].astype(F32), 1.0, 0.0)
        live[q] = alive
        sel_a[q] = alive * (1.0 - to_next)
        sel_b[q] = alive * to_next
        span = (rows, back + rows)
        key = lax.broadcasted_iota(jnp.int32, span, 1).astype(F32) + (base - back)
        query = lax.broadcasted_iota(jnp.int32, span, 0).astype(F32) + base
        allow[q] = jnp.where((key >= doc_start) & (key <= query), 1.0, 0.0)

    @pl.when(r == 0)
    def _():
        halo[...] = jnp.zeros_like(halo)

    gains = gain[...]

    def norm(q):
        @pl.loop(0, rows // 16)
        def _(i):
            part = pl.ds(pl.multiple_of(i * 16, 16), 16)
            values = [xin[q, g, part].astype(F32) for g in range(groups)]
            total = sum(jnp.sum(v * v, axis=1, keepdims=True) for v in values)
            inverse = lax.rsqrt(total * (1.0 / width) + EPSILON)
            for g in range(groups):
                cols = slice(g * WIDE, (g + 1) * WIDE)
                xn[q, part, cols] = (values[g] * inverse * gains[:, cols]).astype(BF)

    def halo_copy(q, g):
        return send(kv.at[q, g], halo.at[q, g, 0], hs.at[q, g], hr.at[q, g], right)

    def relay(q, g):
        return send(new.at[q, g], xin.at[q, g], zs.at[q, g], zr.at[q, g], above)

    def columns(g):
        return pl.ds(pl.multiple_of(g * WIDE, WIDE), WIDE)

    def keep_copy(q, g):
        return pltpu.make_async_copy(
            keep.at[q, g], out.at[0, q, pl.ds(rows, rows), columns(g)], as_.at[q, g]
        )

    def pass_copy(q, g):
        return send(
            pass_on.at[q, g], out.at[0, q, pl.ds(0, rows), columns(g)],
            bs.at[q, g], br.at[q, g], right,
        )

    def weights(g, first, count):
        block = wv[g, :, :, :, :, :, first : first + count]
        return block.reshape(width, count)

    def project_kv(q, g):
        kv[q, g] = jnp.dot(
            xn[q], weights(g, WIDE, 2 * HEAD), preferred_element_type=F32
        ).astype(BF)

        @pl.when(r < ranks - 1)
        def _():
            halo_copy(q, g).start()

    def project_q(q, g):
        qs[q, g] = jnp.dot(
            xn[q], weights(g, 0, WIDE), preferred_element_type=F32
        ).astype(BF)

    def attend(q, g):
        @pl.when(r > 0)
        def _():
            halo_copy(q, g).wait_recv()

        keys = jnp.concatenate([halo[q, g, 0, :, 0:HEAD], kv[q, g, :, 0:HEAD]], axis=0)
        vals = jnp.concatenate([halo[q, g, 0, :, HEAD:], kv[q, g, :, HEAD:]], axis=0)
        for h in range(GROUP):
            cols = slice(h * HEAD, (h + 1) * HEAD)
            scores = lax.dot_general(
                qs[q, g, :, cols], keys, (((1,), (1,)), ((), ())), preferred_element_type=F32
            )
            scores = jnp.where(allow[q] > 0.5, scores * (1.0 / math.sqrt(HEAD)), NEGATIVE)
            highest = jnp.max(scores, axis=1, keepdims=True)
            weighted = jnp.exp(scores - highest)
            totals = jnp.sum(weighted, axis=1, keepdims=True)
            mixed = jnp.dot(weighted.astype(BF), vals, preferred_element_type=F32) / totals
            result = jnp.where(live[q] > 0.5, xin[q, g, :, cols].astype(F32) + mixed, 0.0)
            new[q, g, :, cols] = result.astype(BF)
            keep[q, g, :, cols] = jnp.where(sel_a[q] > 0.5, result, 0.0).astype(BF)
            pass_on[q, g, :, cols] = jnp.where(sel_b[q] > 0.5, result, 0.0).astype(BF)

        @pl.when(z < last_z)
        def _():
            relay(q, g).start()

        keep_copy(q, g).start()

        @pl.when(r < ranks - 1)
        def _():
            pass_copy(q, g).start()

    @pl.when(z == 0)
    def _():
        for q in range(chunks):
            for g in range(groups):
                xin[q, g] = inp[q, :, g * WIDE : (g + 1) * WIDE]

        @pl.loop(0, chunks)
        def _(q):
            norm(q)

    @pl.loop(0, groups)
    def _(g):
        arrive(step1(g))
        start(step2(g))

    def row_steps(g):
        arrive(step2(g))
        start(step3(g))
        start(share(g, 0))

    @pl.loop(0, 2)
    def _(g):
        row_steps(g)

    @pl.loop(0, groups + 1)
    def _(i):
        @pl.when(i < groups)
        def _():
            arrive(step3(i))
            start(step4(i))
            start(share(i, 1))
            start(share(i, 2))

            @pl.when(i + 2 < groups)
            def _():
                row_steps(i + 2)

        @pl.when(i > 0)
        def _():
            g = i - 1
            arrive(step4(g))
            start(share(g, 3))
            for which in range(4):
                arrive(share(g, which))

            @pl.when(z == 0)
            def _():
                @pl.loop(0, chunks)
                def _(q):
                    project_kv(q, g)

                @pl.loop(0, chunks)
                def _(q):
                    project_q(q, g)
                    attend(q, g)

    @pl.when(z > 0)
    def _():
        @pl.loop(0, chunks)
        def _(q):
            @pl.loop(0, groups)
            def _(g):
                relay(q, g).wait_recv()

            norm(q)

            @pl.loop(0, groups)
            def _(g):
                project_kv(q, g)

            @pl.loop(0, groups)
            def _(g):
                project_q(q, g)

            @pl.loop(0, groups)
            def _(g):
                attend(q, g)

    @pl.loop(0, groups)
    def _(g):
        sent(step1(g))
        sent(step2(g))
        sent(step3(g))
        sent(step4(g))
        for which in range(4):
            sent(share(g, which))

    @pl.loop(0, chunks)
    def _(q):
        @pl.loop(0, groups)
        def _(g):
            keep_copy(q, g).wait()

            @pl.when(z < last_z)
            def _():
                relay(q, g).wait_send()

            @pl.when(r < ranks - 1)
            def _():
                halo_copy(q, g).wait_send()
                pass_copy(q, g).wait_send()

            @pl.when(r > 0)
            def _():
                pass_copy(q, g).wait_recv()

            @pl.when(r == 0)
            def _():
                keep[q, g] = jnp.zeros_like(keep[q, g])
                blank = pltpu.make_async_copy(
                    keep.at[q, g], out.at[0, q, pl.ds(0, rows), columns(g)], as_.at[q, g]
                )
                blank.start()
                blank.wait()


def shards(inputs, norm_gain, qkv_weight, batch_lengths, doc_lengths, doc_shift):
    chunks, rows, width = inputs.shape
    groups = KVHEADS
    vmem = pl.BlockSpec(memory_space=pltpu.VMEM)
    smem = pl.BlockSpec(memory_space=pltpu.SMEM)
    dma = pltpu.SemaphoreType.DMA
    state = pltpu.VMEM((chunks, groups, rows, WIDE), BF)
    flags = pltpu.VMEM((chunks, rows, HEAD), F32)
    ring = dma((2, groups, 2))
    piece = dma((chunks, groups))
    return pl.pallas_call(
        kernel,
        out_shape=jax.ShapeDtypeStruct((1, chunks, 2 * rows, width), BF),
        in_specs=[vmem, vmem, vmem, vmem, vmem, smem],
        out_specs=pl.BlockSpec(memory_space=pl.ANY),
        scratch_shapes=[
            pltpu.VMEM((groups, NY, NX, 2, 2, 32, COLS), BF),
            state,
            pltpu.VMEM((chunks, rows, width), BF),
            state,
            state,
            state,
            pltpu.VMEM((chunks, groups, rows, 2 * HEAD), BF),
            pltpu.VMEM((chunks, groups, 1, rows, 2 * HEAD), BF),
            state,
            pltpu.VMEM((chunks, rows, 2 * rows), F32),
            flags,
            flags,
            flags,
            ring, ring, ring, ring, ring, ring, ring, ring,
            dma((2, groups, 4)), dma((2, groups, 4)),
            piece, piece, piece, piece, piece, piece, piece,
        ],
        compiler_params=pltpu.CompilerParams(
            collective_id=0, has_side_effects=True, vmem_limit_bytes=48 << 20
        ),
        name="relay",
    )(inputs, norm_gain, qkv_weight, doc_lengths, doc_shift, batch_lengths)


def solution(mesh):
    placed = (P(None, "cp", None), P("section", None), P("section", "cp", None), P(), P(), P())
    return jax.shard_map(
        shards,
        mesh=mesh,
        in_specs=placed,
        out_specs=P("section", None, "cp", None),
        check_vma=False,
    )
```

```python
import functools
import math

import jax
import jax.numpy as jnp
from jax import lax
from jax.experimental import pallas as pl
from jax.experimental.pallas import tpu as pltpu
from jax.sharding import PartitionSpec as P

MESH = pl.DeviceIdType.MESH
KVHEADS = 4
HEAD = 128
GROUP = 4
WIDE = GROUP * HEAD
COLS = WIDE + 2 * HEAD
NX, NY = 4, 4
EPSILON = 1e-05
NEGATIVE = -1e30
BF, F32 = jnp.bfloat16, jnp.float32


def kernel(
    inp, gain_in, w, lens_in, shifts_in, blen_in, out,
    gain, lens, shifts, blen, fetched, wv, xin, xn, keep, pass_on, kv, halo, qs,
    allow, live, sel_a, sel_b, zero,
    s1s, s1r, s2s, s2r, s3s, s3r, s4s, s4r, ds, dr,
    hs, hr, zs, zr, as_, ar, bs, br, ws, wr, cleared,
):
    z, r = lax.axis_index("section"), lax.axis_index("cp")
    last_z = lax.axis_size("section") - 1
    ranks = lax.axis_size("cp")
    c = r % 2
    x, y = (r // 2) % NX, r // (2 * NX)
    chunks, groups, rows = xin.shape[0], xin.shape[1], xin.shape[2]
    width = groups * WIDE
    back = halo.shape[3]

    def at(dx, dy):
        return (z, (((y + dy) % NY) * NX + (x + dx) % NX) * 2 + c)

    sibling = (z, r + 1 - 2 * c)
    right, left = (r + 1) % ranks, (r + ranks - 1) % ranks

    odd = z % 2
    paired = odd * ((z + last_z - 2) // (last_z + 1))
    gives = (1 - odd) * ((z + last_z - 1) // (last_z + 1))
    works = 1 - gives
    blocks = groups * (works + paired)

    def up(k, rank):
        return ((z + k + last_z + 1) % (last_z + 1), rank)

    following = up(1 + (z + last_z) // (last_z + 1), r)

    barrier = pltpu.get_barrier_semaphore()
    peers = [sibling, at(1, 0), at(3, 0), at(0, 1), at(0, 3), (z, right), (z, left)]
    peers += [up(1, r), up(-1, r), up(2, r), up(-2, r), up(-1, right), up(1, left)]
    for peer in peers:
        pl.semaphore_signal(barrier, inc=1, device_id=peer, device_id_type=MESH)

    for g in range(groups):
        spans = (
            (0, g * WIDE, WIDE),
            (WIDE, width + g * HEAD, HEAD),
            (WIDE + HEAD, width + (groups + g) * HEAD, HEAD),
        )
        for f in range(2):
            for to, first, count in spans:
                pltpu.make_async_copy(
                    w.at[0, pl.ds(32 * f, 32), pl.ds(first, count)],
                    wv.at[g, y, x, c, f, :, pl.ds(to, count)],
                    fetched.at[0],
                ).start()
    small = [
        pltpu.make_async_copy(src, dst, fetched.at[1 + i])
        for i, (src, dst) in enumerate(
            ((lens_in, lens), (shifts_in, shifts), (blen_in, blen), (gain_in, gain.at[0]))
        )
    ]
    for copy in small:
        copy.start()

    @pl.when(z == 0)
    def _():
        for q in range(chunks):
            for g in range(groups):
                pltpu.make_async_copy(
                    inp.at[q, :, pl.ds(g * WIDE, WIDE)], xin.at[q, g], zr.at[q, g]
                ).start()

    mine = wv.at[pl.ds(0, groups), y, x, c]
    pltpu.make_async_copy(mine, mine, fetched.at[0]).wait()
    pl.semaphore_wait(barrier, len(peers))

    def send(src, dst, ss, rs, to):
        return pltpu.make_async_remote_copy(
            src_ref=src, dst_ref=dst, send_sem=ss, recv_sem=rs, device_id=to, device_id_type=MESH
        )

    def same(ref, ss, rs, to):
        return send(ref, ref, ss, rs, to)

    x1, x3, y1, y3 = (x + 1) % NX, (x + 3) % NX, (y + 1) % NY, (y + 3) % NY
    x2, y2 = (x + 2) % NX, (y + 2) % NY
    low, high = pl.ds(0, 16), pl.ds(16, 16)

    def step1(g):
        return [
            same(wv.at[g, y, x, c, 0], s1s.at[0, g, 0], s1r.at[0, g, 0], at(1, 0)),
            same(wv.at[g, y, x, c, 0], s1s.at[0, g, 1], s1r.at[0, g, 1], at(3, 0)),
            same(wv.at[g, y, x, c, 1], s1s.at[1, g, 0], s1r.at[1, g, 0], at(0, 1)),
            same(wv.at[g, y, x, c, 1], s1s.at[1, g, 1], s1r.at[1, g, 1], at(0, 3)),
        ]

    def step2(g):
        return [
            same(wv.at[g, y, x3, c, 0, low], s2s.at[0, g, 0], s2r.at[0, g, 0], at(1, 0)),
            same(wv.at[g, y, x1, c, 0, high], s2s.at[0, g, 1], s2r.at[0, g, 1], at(3, 0)),
            same(wv.at[g, y3, x, c, 1, low], s2s.at[1, g, 0], s2r.at[1, g, 0], at(0, 1)),
            same(wv.at[g, y1, x, c, 1, high], s2s.at[1, g, 1], s2r.at[1, g, 1], at(0, 3)),
        ]

    def step3(g):
        return [
            same(wv.at[g, y, :, c, 0], s3s.at[0, g, 0], s3r.at[0, g, 0], at(0, 1)),
            same(wv.at[g, y, :, c, 0], s3s.at[0, g, 1], s3r.at[0, g, 1], at(0, 3)),
            same(wv.at[g, :, x, c, 1], s3s.at[1, g, 0], s3r.at[1, g, 0], at(1, 0)),
            same(wv.at[g, :, x, c, 1], s3s.at[1, g, 1], s3r.at[1, g, 1], at(3, 0)),
        ]

    def step4(g):
        return [
            same(wv.at[g, y3, :, c, 0, low], s4s.at[0, g, 0], s4r.at[0, g, 0], at(0, 1)),
            same(wv.at[g, y1, :, c, 0, high], s4s.at[0, g, 1], s4r.at[0, g, 1], at(0, 3)),
            same(wv.at[g, :, x3, c, 1, low], s4s.at[1, g, 0], s4r.at[1, g, 0], at(1, 0)),
            same(wv.at[g, :, x1, c, 1, high], s4s.at[1, g, 1], s4r.at[1, g, 1], at(3, 0)),
        ]

    def share(g, which):
        row, col = ((y, x), (y3, x3), (y1, x1), (y2, x2))[which]
        return [
            same(wv.at[g, row, :, c, 0], ds.at[0, g, which], dr.at[0, g, which], sibling),
            same(wv.at[g, :, col, c, 1], ds.at[1, g, which], dr.at[1, g, which], sibling),
        ]

    def start(copies):
        for copy in copies:
            copy.start()

    def arrive(copies):
        for copy in copies:
            copy.wait_recv()

    def sent(copies):
        for copy in copies:
            copy.wait_send()

    @pl.loop(0, groups * works)
    def _(g):
        start(step1(g))

    handed = [
        send(mine, wv.at[pl.ds(groups, groups), y, x, c], ws.at[0], wr.at[0], up(1, r)),
        send(gain.at[0], gain.at[1], ws.at[1], wr.at[1], up(1, r)),
    ]

    @pl.when(gives == 1)
    def _():
        handed[0].start()

    for copy in small:
        copy.wait()

    @pl.when(gives == 1)
    def _():
        handed[1].start()

    spot = lax.broadcasted_iota(jnp.int32, (HEAD, HEAD), 0)
    until = lax.broadcasted_iota(jnp.int32, (HEAD, HEAD), 1)
    upto = jnp.where(spot <= until, 1.0, 0.0).astype(BF)
    length = lens[...].astype(F32)
    ends = jnp.dot(length.astype(BF), upto, preferred_element_type=F32)
    starts = ends - length
    moves = shifts[...].astype(F32)
    base = (r * rows).astype(F32)
    for q in range(chunks):
        begin, end, move = starts[q : q + 1], ends[q : q + 1], moves[q : q + 1]
        place = lax.broadcasted_iota(jnp.int32, (rows, HEAD), 0).astype(F32) + base
        before, after = begin <= place, end > place
        doc_start = jnp.max(jnp.where(before, begin, -1.0), axis=1, keepdims=True)
        doc_end = jnp.min(jnp.where(after, end, 1e9), axis=1, keepdims=True)
        shift = jnp.max(jnp.where(before & after, move, 0.0), axis=1, keepdims=True)
        edge = base + rows
        moved = (doc_start >= base) & (shift > 0.5) & (edge < float(rows) * ranks)
        to_next = jnp.where((doc_end > edge) | moved, 1.0, 0.0)
        alive = jnp.where(place < blen[q].astype(F32), 1.0, 0.0)
        live[q] = alive
        sel_a[q] = alive * (1.0 - to_next)
        sel_b[q] = alive * to_next
        span = (rows, back + rows)
        key = lax.broadcasted_iota(jnp.int32, span, 1).astype(F32) + (base - back)
        query = lax.broadcasted_iota(jnp.int32, span, 0).astype(F32) + base
        allow[q] = jnp.where((key >= doc_start) & (key <= query), 1.0, 0.0)

    @pl.when(r == 0)
    def _():
        halo[...] = jnp.zeros_like(halo)

    def columns(g):
        return pl.ds(pl.multiple_of(g * WIDE, WIDE), WIDE)

    def blank(q, g):
        return pltpu.make_async_copy(
            zero, out.at[0, q, pl.ds(0, rows), columns(g)], cleared.at[0]
        )

    @pl.when(r == 0)
    def _():
        zero[...] = jnp.zeros_like(zero)

        @pl.loop(0, chunks)
        def _(q):
            @pl.loop(0, groups)
            def _(g):
                blank(q, g).start()

    def norm(s, q):
        gains = gain[s]


        @pl.loop(0, rows // 32)
        def _(i):
            part = pl.ds(pl.multiple_of(i * 32, 32), 32)
            values = [xin[q, g, part].astype(F32) for g in range(groups)]
            total = sum(jnp.sum(v * v, axis=1, keepdims=True) for v in values)
            inverse = lax.rsqrt(total * (1.0 / width) + EPSILON)
            for g in range(groups):
                cols = slice(g * WIDE, (g + 1) * WIDE)
                xn[part, cols] = (values[g] * inverse * gains[:, cols]).astype(BF)

    def halo_copy(t, g):
        return send(kv.at[t, g], halo.at[t, g, 0], hs.at[t, g], hr.at[t, g], (z, right))

    def relay(q, g):
        return send(xin.at[q, g], xin.at[q, g], zs.at[q, g], zr.at[q, g], following)

    def keep_local(q, g):
        return pltpu.make_async_copy(
            keep.at[q, g], out.at[0, q, pl.ds(rows, rows), columns(g)], ar.at[q, g]
        )

    def keep_below(q, g):
        return send(
            keep.at[chunks + q, g], out.at[0, q, pl.ds(rows, rows), columns(g)],
            as_.at[q, g], ar.at[q, g], up(-1, r),
        )

    def pass_copy(s, q, g):
        return send(
            pass_on.at[s * chunks + q, g], out.at[0, q, pl.ds(0, rows), columns(g)],
            bs.at[s * chunks + q, g], br.at[q, g], up(-s, right),
        )

    def weights(s, g, first, count):
        block = wv[s * groups + g, :, :, :, :, :, first : first + count]
        return block.reshape(width, count)

    def project_kv(s, q, g):
        t = s * chunks + q
        kv[t, g] = jnp.dot(
            xn[...], weights(s, g, WIDE, 2 * HEAD), preferred_element_type=F32
        ).astype(BF)

        @pl.when(r < ranks - 1)
        def _():
            halo_copy(t, g).start()

    def project_q(s, g):
        qs[g] = jnp.dot(xn[...], weights(s, g, 0, WIDE), preferred_element_type=F32).astype(BF)

    def attend(s, q, g):
        t = s * chunks + q

        @pl.when(r > 0)
        def _():
            halo_copy(t, g).wait_recv()

        keys = jnp.concatenate([halo[t, g, 0, :, 0:HEAD], kv[t, g, :, 0:HEAD]], axis=0)
        vals = jnp.concatenate([halo[t, g, 0, :, HEAD:], kv[t, g, :, HEAD:]], axis=0)
        seen, alive = allow[q] > 0.5, live[q] > 0.5
        heads = [slice(h * HEAD, (h + 1) * HEAD) for h in range(GROUP)]
        scores = [
            lax.dot_general(
                qs[g, :, cols], keys, (((1,), (1,)), ((), ())), preferred_element_type=F32
            )
            for cols in heads
        ]
        scores = [jnp.where(seen, s * (1.0 / math.sqrt(HEAD)), NEGATIVE) for s in scores]
        highest = [jnp.max(s, axis=1, keepdims=True) for s in scores]
        weighted = [jnp.exp(s - m) for s, m in zip(scores, highest)]
        totals = [jnp.sum(e, axis=1, keepdims=True) for e in weighted]
        mixed = [jnp.dot(e.astype(BF), vals, preferred_element_type=F32) for e in weighted]
        for cols, mix, total in zip(heads, mixed, totals):
            result = jnp.where(alive, xin[q, g, :, cols].astype(F32) + mix / total, 0.0)
            xin[q, g, :, cols] = result.astype(BF)

        @pl.when((s == 0) & (z < last_z))
        def _():
            relay(q, g).start()

        for cols in heads:
            result = xin[q, g, :, cols]
            keep[t, g, :, cols] = jnp.where(sel_a[q] > 0.5, result, 0.0).astype(BF)
            pass_on[t, g, :, cols] = jnp.where(sel_b[q] > 0.5, result, 0.0).astype(BF)

        @pl.when(s == 0)
        def _():
            keep_local(q, g).start()

        @pl.when(s == 1)
        def _():
            keep_below(q, g).start()

        @pl.when(r < ranks - 1)
        def _():
            pass_copy(s, q, g).start()

    def take(q):
        @pl.loop(0, groups)
        def _(g):
            relay(q, g).wait_recv()

    @pl.loop(0, groups * works)
    def _(g):
        arrive(step1(g))
        start(step2(g))

    @pl.when(paired == 1)
    def _():
        handed[0].wait_recv()

        @pl.loop(groups, 2 * groups)
        def _(g):
            start(step1(g))

    def row_steps(g):
        arrive(step2(g))
        start(step3(g))
        start(share(g, 0))

    @pl.loop(0, 2 * works)
    def _(g):
        row_steps(g)

    @pl.loop(0, blocks + works)
    def _(i):
        @pl.when(i < blocks)
        def _():
            arrive(step3(i))
            start(step4(i))
            start(share(i, 1))
            start(share(i, 2))

            @pl.when(i + 2 < blocks)
            def _():
                row_steps(i + 2)

            @pl.when(i + groups < blocks)
            def _():
                arrive(step1(i + groups))
                start(step2(i + groups))

        @pl.when(i > 0)
        def _():
            g = i - 1
            arrive(step4(g))
            start(share(g, 3))
            for which in range(4):
                arrive(share(g, which))

            @pl.when((z == 0) & (g == 0))
            def _():
                take(0)
                norm(0, 0)

            @pl.when(z == 0)
            def _():
                project_kv(0, 0, g)
                project_q(0, g)
                attend(0, 0, g)

    @pl.when(paired == 1)
    def _():
        handed[1].wait_recv()

    @pl.loop(1 - (z + last_z) // (last_z + 1), chunks * works)
    def _(q):
        take(q)

        @pl.loop(0, 1 + paired)
        def _(k):
            s = paired - k
            norm(s, q)
            for g in range(groups):
                project_kv(s, q, g)
            for g in range(groups):
                project_q(s, g)

            @pl.loop(0, groups)
            def _(g):
                attend(s, q, g)

    @pl.loop(0, blocks)
    def _(g):
        sent(step1(g))
        sent(step2(g))
        sent(step3(g))
        sent(step4(g))
        for which in range(4):
            sent(share(g, which))

    @pl.when(gives == 1)
    def _():
        sent(handed)

    @pl.loop(0, chunks)
    def _(q):
        @pl.loop(0, groups)
        def _(g):
            @pl.loop(0, works + paired)
            def _(s):
                @pl.when(r < ranks - 1)
                def _():
                    halo_copy(s * chunks + q, g).wait_send()
                    pass_copy(s, q, g).wait_send()

            @pl.when(paired == 1)
            def _():
                keep_below(q, g).wait_send()

            @pl.when((works == 1) & (z < last_z))
            def _():
                relay(q, g).wait_send()

            keep_below(q, g).wait_recv()

            @pl.when(r > 0)
            def _():
                pass_copy(0, q, g).wait_recv()

    @pl.when(r == 0)
    def _():
        first = out.at[0, :, pl.ds(0, rows)]
        pltpu.make_async_copy(first, first, cleared.at[0]).wait()


def shards(inputs, norm_gain, qkv_weight, batch_lengths, doc_lengths, doc_shift):
    chunks, rows, width = inputs.shape
    groups = KVHEADS
    there = pl.BlockSpec(memory_space=pl.ANY)
    dma = pltpu.SemaphoreType.DMA
    state = pltpu.VMEM((chunks, groups, rows, WIDE), BF)
    flags = pltpu.VMEM((chunks, rows, HEAD), F32)
    both = pltpu.VMEM((2 * chunks, groups, rows, WIDE), BF)
    ring = dma((2, 2 * groups, 2))
    piece, tasks = dma((chunks, groups)), dma((2 * chunks, groups))
    return pl.pallas_call(
        kernel,
        out_shape=jax.ShapeDtypeStruct((1, chunks, 2 * rows, width), BF),
        in_specs=[there] * 6,
        out_specs=there,
        scratch_shapes=[
            pltpu.VMEM((2,) + norm_gain.shape, F32),
            pltpu.VMEM(doc_lengths.shape, jnp.int32),
            pltpu.VMEM(doc_shift.shape, jnp.int32),
            pltpu.SMEM(batch_lengths.shape, jnp.int32),
            dma((5,)),
            pltpu.VMEM((2 * groups, NY, NX, 2, 2, 32, COLS), BF),
            state,
            pltpu.VMEM((rows, width), BF),
            both,
            both,
            pltpu.VMEM((2 * chunks, groups, rows, 2 * HEAD), BF),
            pltpu.VMEM((2 * chunks, groups, 1, rows, 2 * HEAD), BF),
            pltpu.VMEM((groups, rows, WIDE), BF),
            pltpu.VMEM((chunks, rows, 2 * rows), F32),
            flags,
            flags,
            flags,
            pltpu.VMEM((rows, WIDE), BF),
            ring, ring, ring, ring, ring, ring, ring, ring,
            dma((2, 2 * groups, 4)), dma((2, 2 * groups, 4)),
            tasks, tasks, piece, piece, piece, piece, tasks, piece,
            dma((2,)), dma((2,)), dma((1,)),
        ],
        compiler_params=pltpu.CompilerParams(
            collective_id=0, has_side_effects=True, vmem_limit_bytes=48 << 20
        ),
        name="relay",
    )(inputs, norm_gain, qkv_weight, doc_lengths, doc_shift, batch_lengths)


def solution(mesh):
    placed = (P(None, "cp", None), P("section", None), P("section", "cp", None), P(), P(), P())
    return jax.shard_map(
        shards,
        mesh=mesh,
        in_specs=placed,
        out_specs=P("section", None, "cp", None),
        check_vma=False,
    )
```

```python
import functools
import math

import jax
import jax.numpy as jnp
from jax import lax
from jax.experimental import pallas as pl
from jax.experimental.pallas import tpu as pltpu
from jax.sharding import PartitionSpec as P

MESH = pl.DeviceIdType.MESH
KVHEADS = 4
HEAD = 128
GROUP = 4
WIDE = GROUP * HEAD
COLS = WIDE + 2 * HEAD
NX, NY = 4, 4
EPSILON = 1e-05
NEGATIVE = -1e30
BF, F32 = jnp.bfloat16, jnp.float32


def kernel(
    inp, gain_in, w, lens_in, shifts_in, blen_in, out,
    gain, lens, shifts, blen, fetched, wv, xin, xn, raw, keep, pass_on, kv, halo, qs,
    allow, live, sel_a, sel_b, zero,
    s1s, s1r, s2s, s2r, s3s, s3r, s4s, s4r, ds, dr,
    hs, hr, zs, zr, as_, ar, bs, br, ws, wr, cleared,
):
    z, r = lax.axis_index("section"), lax.axis_index("cp")
    last_z = lax.axis_size("section") - 1
    ranks = lax.axis_size("cp")
    c = r % 2
    x, y = (r // 2) % NX, r // (2 * NX)
    chunks, groups, rows = xin.shape[0], xin.shape[1], xin.shape[2]
    width = groups * WIDE
    back = halo.shape[3]

    def at(dx, dy):
        return (z, (((y + dy) % NY) * NX + (x + dx) % NX) * 2 + c)

    sibling = (z, r + 1 - 2 * c)
    right, left = (r + 1) % ranks, (r + ranks - 1) % ranks

    odd = z % 2
    paired = odd * ((z + last_z - 2) // (last_z + 1))
    gives = (1 - odd) * ((z + last_z - 1) // (last_z + 1))
    works = 1 - gives
    blocks = groups * (works + paired)

    def up(k, rank):
        return ((z + k + last_z + 1) % (last_z + 1), rank)

    following = up(1 + (z + last_z) // (last_z + 1), r)

    barrier = pltpu.get_barrier_semaphore()
    peers = [sibling, at(1, 0), at(3, 0), at(0, 1), at(0, 3), (z, right), (z, left)]
    peers += [up(1, r), up(-1, r), up(2, r), up(-2, r)]
    for peer in peers:
        pl.semaphore_signal(barrier, inc=1, device_id=peer, device_id_type=MESH)

    for g in range(groups):
        spans = (
            (0, g * WIDE, WIDE),
            (WIDE, width + g * HEAD, HEAD),
            (WIDE + HEAD, width + (groups + g) * HEAD, HEAD),
        )
        for f in range(2):
            for to, first, count in spans:
                pltpu.make_async_copy(
                    w.at[0, pl.ds(32 * f, 32), pl.ds(first, count)],
                    wv.at[g, y, x, c, f, :, pl.ds(to, count)],
                    fetched.at[0],
                ).start()
    small = [
        pltpu.make_async_copy(src, dst, fetched.at[1 + i])
        for i, (src, dst) in enumerate(
            ((lens_in, lens), (shifts_in, shifts), (blen_in, blen), (gain_in, gain.at[0]))
        )
    ]
    for copy in small:
        copy.start()

    @pl.when(z == 0)
    def _():
        for q in range(chunks):
            for g in range(groups):
                pltpu.make_async_copy(
                    inp.at[q, :, pl.ds(g * WIDE, WIDE)], xin.at[q, g], zr.at[q, g]
                ).start()

    mine = wv.at[pl.ds(0, groups), y, x, c]
    pltpu.make_async_copy(mine, mine, fetched.at[0]).wait()
    pl.semaphore_wait(barrier, len(peers))

    def send(src, dst, ss, rs, to):
        return pltpu.make_async_remote_copy(
            src_ref=src, dst_ref=dst, send_sem=ss, recv_sem=rs, device_id=to, device_id_type=MESH
        )

    def same(ref, ss, rs, to):
        return send(ref, ref, ss, rs, to)

    x1, x3, y1, y3 = (x + 1) % NX, (x + 3) % NX, (y + 1) % NY, (y + 3) % NY
    x2, y2 = (x + 2) % NX, (y + 2) % NY
    low, high = pl.ds(0, 16), pl.ds(16, 16)

    def step1(g):
        return [
            same(wv.at[g, y, x, c, 0], s1s.at[0, g, 0], s1r.at[0, g, 0], at(1, 0)),
            same(wv.at[g, y, x, c, 0], s1s.at[0, g, 1], s1r.at[0, g, 1], at(3, 0)),
            same(wv.at[g, y, x, c, 1], s1s.at[1, g, 0], s1r.at[1, g, 0], at(0, 1)),
            same(wv.at[g, y, x, c, 1], s1s.at[1, g, 1], s1r.at[1, g, 1], at(0, 3)),
        ]

    def step2(g):
        return [
            same(wv.at[g, y, x3, c, 0, low], s2s.at[0, g, 0], s2r.at[0, g, 0], at(1, 0)),
            same(wv.at[g, y, x1, c, 0, high], s2s.at[0, g, 1], s2r.at[0, g, 1], at(3, 0)),
            same(wv.at[g, y3, x, c, 1, low], s2s.at[1, g, 0], s2r.at[1, g, 0], at(0, 1)),
            same(wv.at[g, y1, x, c, 1, high], s2s.at[1, g, 1], s2r.at[1, g, 1], at(0, 3)),
        ]

    def step3(g):
        return [
            same(wv.at[g, y, :, c, 0], s3s.at[0, g, 0], s3r.at[0, g, 0], at(0, 1)),
            same(wv.at[g, y, :, c, 0], s3s.at[0, g, 1], s3r.at[0, g, 1], at(0, 3)),
            same(wv.at[g, :, x, c, 1], s3s.at[1, g, 0], s3r.at[1, g, 0], at(1, 0)),
            same(wv.at[g, :, x, c, 1], s3s.at[1, g, 1], s3r.at[1, g, 1], at(3, 0)),
        ]

    def step4(g):
        return [
            same(wv.at[g, y3, :, c, 0, low], s4s.at[0, g, 0], s4r.at[0, g, 0], at(0, 1)),
            same(wv.at[g, y1, :, c, 0, high], s4s.at[0, g, 1], s4r.at[0, g, 1], at(0, 3)),
            same(wv.at[g, :, x3, c, 1, low], s4s.at[1, g, 0], s4r.at[1, g, 0], at(1, 0)),
            same(wv.at[g, :, x1, c, 1, high], s4s.at[1, g, 1], s4r.at[1, g, 1], at(3, 0)),
        ]

    def share(g, which):
        row, col = ((y, x), (y3, x3), (y1, x1), (y2, x2))[which]
        return [
            same(wv.at[g, row, :, c, 0], ds.at[0, g, which], dr.at[0, g, which], sibling),
            same(wv.at[g, :, col, c, 1], ds.at[1, g, which], dr.at[1, g, which], sibling),
        ]

    def start(copies):
        for copy in copies:
            copy.start()

    def arrive(copies):
        for copy in copies:
            copy.wait_recv()

    def sent(copies):
        for copy in copies:
            copy.wait_send()

    @pl.loop(0, groups * works)
    def _(g):
        start(step1(g))

    handed = [
        send(mine, wv.at[pl.ds(groups, groups), y, x, c], ws.at[0], wr.at[0], up(1, r)),
        send(gain.at[0], gain.at[1], ws.at[1], wr.at[1], up(1, r)),
    ]

    @pl.when(gives == 1)
    def _():
        handed[0].start()

    for copy in small:
        copy.wait()

    @pl.when(gives == 1)
    def _():
        handed[1].start()

    spot = lax.broadcasted_iota(jnp.int32, (HEAD, HEAD), 0)
    until = lax.broadcasted_iota(jnp.int32, (HEAD, HEAD), 1)
    upto = jnp.where(spot <= until, 1.0, 0.0).astype(BF)
    length = lens[...].astype(F32)
    ends = jnp.dot(length.astype(BF), upto, preferred_element_type=F32)
    starts = ends - length
    moves = shifts[...].astype(F32)
    base = (r * rows).astype(F32)
    for q in range(chunks):
        begin, end, move = starts[q : q + 1], ends[q : q + 1], moves[q : q + 1]
        place = lax.broadcasted_iota(jnp.int32, (rows, HEAD), 0).astype(F32) + base
        before, after = begin <= place, end > place
        doc_start = jnp.max(jnp.where(before, begin, -1.0), axis=1, keepdims=True)
        doc_end = jnp.min(jnp.where(after, end, 1e9), axis=1, keepdims=True)
        shift = jnp.max(jnp.where(before & after, move, 0.0), axis=1, keepdims=True)
        edge = base + rows
        moved = (doc_start >= base) & (shift > 0.5) & (edge < float(rows) * ranks)
        to_next = jnp.where((doc_end > edge) | moved, 1.0, 0.0)
        alive = jnp.where(place < blen[q].astype(F32), 1.0, 0.0)
        live[q] = alive
        sel_a[q] = alive * (1.0 - to_next)
        sel_b[q] = alive * to_next
        span = (rows, back + rows)
        key = lax.broadcasted_iota(jnp.int32, span, 1).astype(F32) + (base - back)
        query = lax.broadcasted_iota(jnp.int32, span, 0).astype(F32) + base
        allow[q] = jnp.where((key >= doc_start) & (key <= query), 1.0, 0.0)

    @pl.when(r == 0)
    def _():
        halo[...] = jnp.zeros_like(halo)

    def columns(g):
        return pl.ds(pl.multiple_of(g * WIDE, WIDE), WIDE)

    def blank(q, g):
        return pltpu.make_async_copy(
            zero, out.at[0, q, pl.ds(0, rows), columns(g)], cleared.at[0]
        )

    @pl.when(r == 0)
    def _():
        zero[...] = jnp.zeros_like(zero)

        @pl.loop(0, chunks)
        def _(q):
            @pl.loop(0, groups)
            def _(g):
                blank(q, g).start()

    def norm(s, q):
        gains = gain[s]


        @pl.loop(0, rows // 32)
        def _(i):
            part = pl.ds(pl.multiple_of(i * 32, 32), 32)
            values = [xin[q, g, part].astype(F32) for g in range(groups)]
            total = sum(jnp.sum(v * v, axis=1, keepdims=True) for v in values)
            inverse = lax.rsqrt(total * (1.0 / width) + EPSILON)
            for g in range(groups):
                cols = slice(g * WIDE, (g + 1) * WIDE)
                xn[part, cols] = (values[g] * inverse * gains[:, cols]).astype(BF)

    def halo_copy(t, g):
        return send(kv.at[t, g], halo.at[t, g, 0], hs.at[t, g], hr.at[t, g], (z, right))

    def relay(q, g):
        return send(xin.at[q, g], xin.at[q, g], zs.at[q, g], zr.at[q, g], following)

    def hand_back(q, g):
        return send(raw.at[q, g], xin.at[q, g], as_.at[q, g], zr.at[q, g], up(-1, r))

    def keep_copy(q, g):
        return pltpu.make_async_copy(
            keep.at[q, g], out.at[0, q, pl.ds(rows, rows), columns(g)], ar.at[q, g]
        )

    def pass_copy(q, g):
        return send(
            pass_on.at[q, g], out.at[0, q, pl.ds(0, rows), columns(g)],
            bs.at[q, g], br.at[q, g], (z, right),
        )

    def deliver(q, g):
        for h in range(GROUP):
            cols = slice(h * HEAD, (h + 1) * HEAD)
            result = xin[q, g, :, cols]
            keep[q, g, :, cols] = jnp.where(sel_a[q] > 0.5, result, 0.0).astype(BF)
            pass_on[q, g, :, cols] = jnp.where(sel_b[q] > 0.5, result, 0.0).astype(BF)
        keep_copy(q, g).start()

        @pl.when(r < ranks - 1)
        def _():
            pass_copy(q, g).start()

    def weights(s, g, first, count):
        block = wv[s * groups + g, :, :, :, :, :, first : first + count]
        return block.reshape(width, count)

    def project_kv(s, q, g):
        t = s * chunks + q
        kv[t, g] = jnp.dot(
            xn[...], weights(s, g, WIDE, 2 * HEAD), preferred_element_type=F32
        ).astype(BF)

        @pl.when(r < ranks - 1)
        def _():
            halo_copy(t, g).start()

    def project_q(s, g):
        qs[g] = jnp.dot(xn[...], weights(s, g, 0, WIDE), preferred_element_type=F32).astype(BF)

    def attend(s, q, g):
        t = s * chunks + q

        @pl.when(r > 0)
        def _():
            halo_copy(t, g).wait_recv()

        keys = jnp.concatenate([halo[t, g, 0, :, 0:HEAD], kv[t, g, :, 0:HEAD]], axis=0)
        vals = jnp.concatenate([halo[t, g, 0, :, HEAD:], kv[t, g, :, HEAD:]], axis=0)
        seen, alive = allow[q] > 0.5, live[q] > 0.5
        heads = [slice(h * HEAD, (h + 1) * HEAD) for h in range(GROUP)]
        scores = [
            lax.dot_general(
                qs[g, :, cols], keys, (((1,), (1,)), ((), ())), preferred_element_type=F32
            )
            for cols in heads
        ]
        scores = [jnp.where(seen, s * (1.0 / math.sqrt(HEAD)), NEGATIVE) for s in scores]
        highest = [jnp.max(s, axis=1, keepdims=True) for s in scores]
        weighted = [jnp.exp(s - m) for s, m in zip(scores, highest)]
        totals = [jnp.sum(e, axis=1, keepdims=True) for e in weighted]
        mixed = [jnp.dot(e.astype(BF), vals, preferred_element_type=F32) for e in weighted]
        for cols, mix, total in zip(heads, mixed, totals):
            result = jnp.where(alive, xin[q, g, :, cols].astype(F32) + mix / total, 0.0)
            xin[q, g, :, cols] = result.astype(BF)

        @pl.when((s == 0) & (z < last_z))
        def _():
            relay(q, g).start()

        @pl.when(s == 1)
        def _():
            raw[q, g] = xin[q, g]
            hand_back(q, g).start()

        @pl.when((s == 0) & (z == last_z))
        def _():
            deliver(q, g)

    def take(q):
        @pl.loop(0, groups)
        def _(g):
            relay(q, g).wait_recv()

    @pl.loop(0, groups * works)
    def _(g):
        arrive(step1(g))
        start(step2(g))

    @pl.when(paired == 1)
    def _():
        handed[0].wait_recv()

        @pl.loop(groups, 2 * groups)
        def _(g):
            start(step1(g))

    def row_steps(g):
        arrive(step2(g))
        start(step3(g))
        start(share(g, 0))

    @pl.loop(0, 2 * works)
    def _(g):
        row_steps(g)

    @pl.loop(0, blocks + works)
    def _(i):
        @pl.when(i < blocks)
        def _():
            arrive(step3(i))
            start(step4(i))
            start(share(i, 1))
            start(share(i, 2))

            @pl.when(i + 2 < blocks)
            def _():
                row_steps(i + 2)

            @pl.when(i + groups < blocks)
            def _():
                arrive(step1(i + groups))
                start(step2(i + groups))

        @pl.when(i > 0)
        def _():
            g = i - 1
            arrive(step4(g))
            start(share(g, 3))
            for which in range(4):
                arrive(share(g, which))

            @pl.when((z == 0) & (g == 0))
            def _():
                take(0)
                norm(0, 0)

            @pl.when(z == 0)
            def _():
                project_kv(0, 0, g)
                project_q(0, g)
                attend(0, 0, g)

    @pl.when(paired == 1)
    def _():
        handed[1].wait_recv()

    @pl.loop(1 - (z + last_z) // (last_z + 1), chunks * works)
    def _(q):
        take(q)

        @pl.loop(0, 1 + paired)
        def _(k):
            s = paired - k
            norm(s, q)
            for g in range(groups):
                project_kv(s, q, g)
            for g in range(groups):
                project_q(s, g)

            @pl.loop(0, groups)
            def _(g):
                attend(s, q, g)

    @pl.when(z < last_z)
    def _():
        @pl.loop(0, chunks)
        def _(q):
            @pl.loop(0, groups)
            def _(g):
                @pl.when(gives == 1)
                def _():
                    hand_back(q, g).wait_recv()

                deliver(q, g)

    @pl.loop(0, blocks)
    def _(g):
        sent(step1(g))
        sent(step2(g))
        sent(step3(g))
        sent(step4(g))
        for which in range(4):
            sent(share(g, which))

    @pl.when(gives == 1)
    def _():
        sent(handed)

    @pl.loop(0, chunks)
    def _(q):
        @pl.loop(0, groups)
        def _(g):
            @pl.when(r < ranks - 1)
            def _():
                @pl.loop(0, works + paired)
                def _(s):
                    halo_copy(s * chunks + q, g).wait_send()

                pass_copy(q, g).wait_send()

            @pl.when(paired == 1)
            def _():
                hand_back(q, g).wait_send()

            @pl.when((works == 1) & (z < last_z))
            def _():
                relay(q, g).wait_send()

            keep_copy(q, g).wait()

            @pl.when(r > 0)
            def _():
                pass_copy(q, g).wait_recv()

    @pl.when(r == 0)
    def _():
        first = out.at[0, :, pl.ds(0, rows)]
        pltpu.make_async_copy(first, first, cleared.at[0]).wait()


def shards(inputs, norm_gain, qkv_weight, batch_lengths, doc_lengths, doc_shift):
    chunks, rows, width = inputs.shape
    groups = KVHEADS
    there = pl.BlockSpec(memory_space=pl.ANY)
    dma = pltpu.SemaphoreType.DMA
    state = pltpu.VMEM((chunks, groups, rows, WIDE), BF)
    flags = pltpu.VMEM((chunks, rows, HEAD), F32)
    ring = dma((2, 2 * groups, 2))
    piece, tasks = dma((chunks, groups)), dma((2 * chunks, groups))
    return pl.pallas_call(
        kernel,
        out_shape=jax.ShapeDtypeStruct((1, chunks, 2 * rows, width), BF),
        in_specs=[there] * 6,
        out_specs=there,
        scratch_shapes=[
            pltpu.VMEM((2,) + norm_gain.shape, F32),
            pltpu.VMEM(doc_lengths.shape, jnp.int32),
            pltpu.VMEM(doc_shift.shape, jnp.int32),
            pltpu.SMEM(batch_lengths.shape, jnp.int32),
            dma((5,)),
            pltpu.VMEM((2 * groups, NY, NX, 2, 2, 32, COLS), BF),
            state,
            pltpu.VMEM((rows, width), BF),
            state,
            state,
            state,
            pltpu.VMEM((2 * chunks, groups, rows, 2 * HEAD), BF),
            pltpu.VMEM((2 * chunks, groups, 1, rows, 2 * HEAD), BF),
            pltpu.VMEM((groups, rows, WIDE), BF),
            pltpu.VMEM((chunks, rows, 2 * rows), F32),
            flags,
            flags,
            flags,
            pltpu.VMEM((rows, WIDE), BF),
            ring, ring, ring, ring, ring, ring, ring, ring,
            dma((2, 2 * groups, 4)), dma((2, 2 * groups, 4)),
            tasks, tasks, piece, piece, piece, piece, piece, piece,
            dma((2,)), dma((2,)), dma((1,)),
        ],
        compiler_params=pltpu.CompilerParams(
            collective_id=0, has_side_effects=True, vmem_limit_bytes=48 << 20
        ),
        name="relay",
    )(inputs, norm_gain, qkv_weight, doc_lengths, doc_shift, batch_lengths)


def solution(mesh):
    placed = (P(None, "cp", None), P("section", None), P("section", "cp", None), P(), P(), P())
    return jax.shard_map(
        shards,
        mesh=mesh,
        in_specs=placed,
        out_specs=P("section", None, "cp", None),
        check_vma=False,
    )
```

```python
import functools
import math

import jax
import jax.numpy as jnp
from jax import lax
from jax.experimental import pallas as pl
from jax.experimental.pallas import tpu as pltpu
from jax.sharding import PartitionSpec as P

MESH = pl.DeviceIdType.MESH
KVHEADS = 4
HEAD = 128
GROUP = 4
WIDE = GROUP * HEAD
COLS = WIDE + 2 * HEAD
NX, NY = 4, 4
EPSILON = 1e-05
NEGATIVE = -1e30
BF, F32 = jnp.bfloat16, jnp.float32
STEP = 1


def kernel(
    inp, gain_in, w, lens_in, shifts_in, blen_in, out,
    gain, lens, shifts, blen, fetched, wv, xin, xn, raw, keep, pass_on, kv, halo, qs,
    allow, live, sel_a, sel_b, zero,
    s1s, s1r, s2s, s2r, s3s, s3r, s4s, s4r, ds, dr,
    hs, hr, zs, zr, as_, ar, bs, br, ws, wr, cleared,
):
    z, r = lax.axis_index("section"), lax.axis_index("cp")
    last_z = lax.axis_size("section") - 1
    ranks = lax.axis_size("cp")
    c = r % 2
    x, y = (r // 2) % NX, r // (2 * NX)
    chunks, groups, rows = xin.shape[0], xin.shape[1], xin.shape[2]
    width = groups * WIDE
    back, half = rows, rows // 2

    def at(dx, dy):
        return (z, (((y + dy) % NY) * NX + (x + dx) % NX) * 2 + c)

    sibling = (z, r + 1 - 2 * c)
    right, left = (r + 1) % ranks, (r + ranks - 1) % ranks

    odd = z % 2
    paired = odd * ((z + last_z - 2) // (last_z + 1))
    gives = (1 - odd) * ((z + last_z - 1) // (last_z + 1))
    works = 1 - gives
    blocks = groups * works + (groups - 1) * paired + gives

    def up(k, rank):
        return ((z + k + last_z + 1) % (last_z + 1), rank)

    following = up(1 + (z + last_z) // (last_z + 1), r)

    barrier = pltpu.get_barrier_semaphore()
    peers = [sibling, at(1, 0), at(3, 0), at(0, 1), at(0, 3), (z, right), (z, left)]
    peers += [up(1, r), up(-1, r), up(2, r), up(-2, r)]
    for peer in peers:
        pl.semaphore_signal(barrier, inc=1, device_id=peer, device_id_type=MESH)

    def slot(s, g):
        return s * groups + (g + s * (groups - 1)) % groups

    for g in range(groups):
        spans = (
            (0, g * WIDE, WIDE),
            (WIDE, width + g * HEAD, HEAD),
            (WIDE + HEAD, width + (groups + g) * HEAD, HEAD),
        )
        for f in range(2):
            for to, first, count in spans:
                pltpu.make_async_copy(
                    w.at[0, pl.ds(32 * f, 32), pl.ds(first, count)],
                    wv.at[slot(0, g), y, x, c, f, :, pl.ds(to, count)],
                    fetched.at[g],
                ).start()
    small = [
        pltpu.make_async_copy(src, dst, fetched.at[groups + i])
        for i, (src, dst) in enumerate(
            ((lens_in, lens), (shifts_in, shifts), (blen_in, blen), (gain_in, gain.at[0]))
        )
    ]
    for copy in small:
        copy.start()

    @pl.when(z == 0)
    def _():
        for q in range(chunks):
            for g in range(groups):
                pltpu.make_async_copy(
                    inp.at[q, :, pl.ds(g * WIDE, WIDE)], xin.at[q, g], zr.at[q, g]
                ).start()

    mine = wv.at[pl.ds(1, groups - 1), y, x, c]
    for g in range(groups):
        block = wv.at[slot(0, g), y, x, c]
        pltpu.make_async_copy(block, block, fetched.at[g]).wait()
    pl.semaphore_wait(barrier, len(peers))

    def send(src, dst, ss, rs, to):
        return pltpu.make_async_remote_copy(
            src_ref=src, dst_ref=dst, send_sem=ss, recv_sem=rs, device_id=to, device_id_type=MESH
        )

    def same(ref, ss, rs, to):
        return send(ref, ref, ss, rs, to)

    x1, x3, y1, y3 = (x + 1) % NX, (x + 3) % NX, (y + 1) % NY, (y + 3) % NY
    x2, y2 = (x + 2) % NX, (y + 2) % NY
    low, high = pl.ds(0, 16), pl.ds(16, 16)

    def step1(g):
        return [
            same(wv.at[g, y, x, c, 0], s1s.at[0, g, 0], s1r.at[0, g, 0], at(1, 0)),
            same(wv.at[g, y, x, c, 0], s1s.at[0, g, 1], s1r.at[0, g, 1], at(3, 0)),
            same(wv.at[g, y, x, c, 1], s1s.at[1, g, 0], s1r.at[1, g, 0], at(0, 1)),
            same(wv.at[g, y, x, c, 1], s1s.at[1, g, 1], s1r.at[1, g, 1], at(0, 3)),
        ]

    def step2(g):
        return [
            same(wv.at[g, y, x3, c, 0, low], s2s.at[0, g, 0], s2r.at[0, g, 0], at(1, 0)),
            same(wv.at[g, y, x1, c, 0, high], s2s.at[0, g, 1], s2r.at[0, g, 1], at(3, 0)),
            same(wv.at[g, y3, x, c, 1, low], s2s.at[1, g, 0], s2r.at[1, g, 0], at(0, 1)),
            same(wv.at[g, y1, x, c, 1, high], s2s.at[1, g, 1], s2r.at[1, g, 1], at(0, 3)),
        ]

    def step3(g):
        return [
            same(wv.at[g, y, :, c, 0], s3s.at[0, g, 0], s3r.at[0, g, 0], at(0, 1)),
            same(wv.at[g, y, :, c, 0], s3s.at[0, g, 1], s3r.at[0, g, 1], at(0, 3)),
            same(wv.at[g, :, x, c, 1], s3s.at[1, g, 0], s3r.at[1, g, 0], at(1, 0)),
            same(wv.at[g, :, x, c, 1], s3s.at[1, g, 1], s3r.at[1, g, 1], at(3, 0)),
        ]

    def step4(g):
        return [
            same(wv.at[g, y3, :, c, 0, low], s4s.at[0, g, 0], s4r.at[0, g, 0], at(0, 1)),
            same(wv.at[g, y1, :, c, 0, high], s4s.at[0, g, 1], s4r.at[0, g, 1], at(0, 3)),
            same(wv.at[g, :, x3, c, 1, low], s4s.at[1, g, 0], s4r.at[1, g, 0], at(1, 0)),
            same(wv.at[g, :, x1, c, 1, high], s4s.at[1, g, 1], s4r.at[1, g, 1], at(3, 0)),
        ]

    def share(g, which):
        row, col = ((y, x), (y3, x3), (y1, x1), (y2, x2))[which]
        return [
            same(wv.at[g, row, :, c, 0], ds.at[0, g, which], dr.at[0, g, which], sibling),
            same(wv.at[g, :, col, c, 1], ds.at[1, g, which], dr.at[1, g, which], sibling),
        ]

    def start(copies):
        for copy in copies:
            copy.start()

    def arrive(copies):
        for copy in copies:
            copy.wait_recv()

    def sent(copies):
        for copy in copies:
            copy.wait_send()

    first = works * groups + gives

    @pl.loop(0, first)
    def _(g):
        start(step1(g))

    handed = [
        send(mine, wv.at[pl.ds(groups, groups - 1), y, x, c], ws.at[0], wr.at[0], up(1, r)),
        send(gain.at[0], gain.at[1], ws.at[1], wr.at[1], up(1, r)),
    ]

    @pl.when(gives == 1)
    def _():
        handed[0].start()

    for copy in small:
        copy.wait()

    @pl.when(gives == 1)
    def _():
        handed[1].start()

    spot = lax.broadcasted_iota(jnp.int32, (HEAD, HEAD), 0)
    until = lax.broadcasted_iota(jnp.int32, (HEAD, HEAD), 1)
    upto = jnp.where(spot <= until, 1.0, 0.0).astype(BF)
    length = lens[...].astype(F32)
    ends = jnp.dot(length.astype(BF), upto, preferred_element_type=F32)
    starts = ends - length
    moves = shifts[...].astype(F32)
    base = (r * rows).astype(F32)
    for q in range(chunks):
        begin, end, move = starts[q : q + 1], ends[q : q + 1], moves[q : q + 1]
        place = lax.broadcasted_iota(jnp.int32, (rows, HEAD), 0).astype(F32) + base
        before, after = begin <= place, end > place
        doc_start = jnp.max(jnp.where(before, begin, -1.0), axis=1, keepdims=True)
        doc_end = jnp.min(jnp.where(after, end, 1e9), axis=1, keepdims=True)
        shift = jnp.max(jnp.where(before & after, move, 0.0), axis=1, keepdims=True)
        edge = base + rows
        moved = (doc_start >= base) & (shift > 0.5) & (edge < float(rows) * ranks)
        to_next = jnp.where((doc_end > edge) | moved, 1.0, 0.0)
        alive = jnp.where(place < blen[q].astype(F32), 1.0, 0.0)
        live[q] = alive
        sel_a[q] = alive * (1.0 - to_next)
        sel_b[q] = alive * to_next
        for i in range(2):
            part = slice(i * half, (i + 1) * half)
            span = (half, back + half)
            query = lax.broadcasted_iota(jnp.int32, span, 0).astype(F32) + (base + i * half)
            key = lax.broadcasted_iota(jnp.int32, span, 1).astype(F32) + (base + i * half - back)
            seen = (key >= doc_start[part]) & (key <= query)
            allow[q, i] = jnp.where(seen, 1.0, 0.0)

    @pl.when(r == 0)
    def _():
        halo[...] = jnp.zeros_like(halo)

    def columns(g):
        return pl.ds(pl.multiple_of(g * WIDE, WIDE), WIDE)

    def blank(q, g):
        return pltpu.make_async_copy(
            zero, out.at[0, q, pl.ds(0, rows), columns(g)], cleared.at[0]
        )

    @pl.when(r == 0)
    def _():
        zero[...] = jnp.zeros_like(zero)

        @pl.loop(0, chunks)
        def _(q):
            @pl.loop(0, groups)
            def _(g):
                blank(q, g).start()

    def norm(s, q):
        gains = gain[s]


        @pl.loop(0, rows // half)
        def _(i):
            part = pl.ds(pl.multiple_of(i * half, half), half)
            values = [xin[q, g, part].astype(F32) for g in range(groups)]
            total = sum(jnp.sum(v * v, axis=1, keepdims=True) for v in values)
            inverse = lax.rsqrt(total * (1.0 / width) + EPSILON)
            for g in range(groups):
                cols = slice(g * WIDE, (g + 1) * WIDE)
                xn[part, cols] = (values[g] * inverse * gains[:, cols]).astype(BF)

    def halo_copy(t, g):
        return send(kv.at[t, g], halo.at[t, g, 0], hs.at[t, g], hr.at[t, g], (z, right))

    def relay(q, g):
        return send(xin.at[q, g], xin.at[q, g], zs.at[q, g], zr.at[q, g], following)

    def hand_back(q, g):
        return send(raw.at[q, g], xin.at[q, g], as_.at[q, g], zr.at[q, g], up(-1, r))

    def keep_copy(q, g):
        return pltpu.make_async_copy(
            keep.at[q, g], out.at[0, q, pl.ds(rows, rows), columns(g)], ar.at[q, g]
        )

    def pass_copy(q, g):
        return send(
            pass_on.at[q, g], out.at[0, q, pl.ds(0, rows), columns(g)],
            bs.at[q, g], br.at[q, g], (z, right),
        )

    def deliver(q, g):
        for h in range(GROUP):
            cols = slice(h * HEAD, (h + 1) * HEAD)
            result = xin[q, g, :, cols]
            keep[q, g, :, cols] = jnp.where(sel_a[q] > 0.5, result, 0.0).astype(BF)
            pass_on[q, g, :, cols] = jnp.where(sel_b[q] > 0.5, result, 0.0).astype(BF)
        keep_copy(q, g).start()

        @pl.when(r < ranks - 1)
        def _():
            pass_copy(q, g).start()

    def weights(s, g, first, count):
        block = wv[slot(s, g), :, :, :, :, :, first : first + count]
        return block.reshape(width, count)

    def project_kv(s, q, g):
        t = s * chunks + q
        kv[t, g] = jnp.dot(
            xn[...], weights(s, g, WIDE, 2 * HEAD), preferred_element_type=F32
        ).astype(BF)

        @pl.when(r < ranks - 1)
        def _():
            halo_copy(t, g).start()

    def project_q(s, g):
        qs[g] = jnp.dot(xn[...], weights(s, g, 0, WIDE), preferred_element_type=F32).astype(BF)

    heads = [slice(h * HEAD, (h + 1) * HEAD) for h in range(GROUP)]
    parts = [slice(i * half, (i + 1) * half) for i in range(2)]

    def attend(s, q, some):
        t = s * chunks + q
        for g in some:

            @pl.when(r > 0)
            def _():
                halo_copy(t, g).wait_recv()

        def seen_rows(g, i, cols):
            earlier, own = halo[t, g, 0, i * half :, cols], kv[t, g, : (i + 1) * half, cols]
            return jnp.concatenate([earlier, own], axis=0)

        tiles = [(g, i) for g in some for i in range(2)]
        seen = [jnp.concatenate([allow[q, i] > 0.5] * GROUP, axis=0) for i in range(2)]
        ones = jnp.ones((back + half, HEAD), BF)
        scores = [
            lax.dot_general(
                jnp.concatenate([qs[g, parts[i], cols] for cols in heads], axis=0),
                seen_rows(g, i, heads[0]),
                (((1,), (1,)), ((), ())),
                preferred_element_type=F32,
            )
            for g, i in tiles
        ]
        scores = [jnp.where(seen[i], a, NEGATIVE) for (_, i), a in zip(tiles, scores)]
        highest = [jnp.max(a, axis=1, keepdims=True) for a in scores]
        scale = math.log2(math.e) / math.sqrt(HEAD)
        weighted = [jnp.exp2((a - m) * scale).astype(BF) for a, m in zip(scores, highest)]
        mixed = [
            jnp.dot(
                e, jnp.concatenate([seen_rows(g, i, heads[1]), ones], axis=1),
                preferred_element_type=F32,
            )
            for (g, i), e in zip(tiles, weighted)
        ]
        for (g, i), mix in zip(tiles, mixed):
            mix = mix[:, :HEAD] / mix[:, HEAD:]
            alive = live[q, parts[i]] > 0.5
            for h, cols in enumerate(heads):
                more = mix[h * half : (h + 1) * half]
                result = jnp.where(alive, xin[q, g, parts[i], cols].astype(F32) + more, 0.0)
                xin[q, g, parts[i], cols] = result.astype(BF)

        for g in some:
            send_on(s, q, g)

    def send_on(s, q, g):
        @pl.when((s == 0) & (z < last_z))
        def _():
            relay(q, g).start()

        @pl.when(s == 1)
        def _():
            raw[q, g] = xin[q, g]
            hand_back(q, g).start()

        @pl.when((s == 0) & (z == last_z))
        def _():
            deliver(q, g)

    def take(q):
        @pl.loop(0, groups)
        def _(g):
            relay(q, g).wait_recv()

    def layer(s, q):
        norm(s, q)
        for g in range(groups):
            project_kv(s, q, g)
        for g in range(groups):
            project_q(s, g)

        @pl.loop(0, groups // STEP)
        def _(g):
            attend(s, q, tuple(g * STEP + i for i in range(STEP)))

    @pl.when(paired == 1)
    def _():
        handed[0].wait_recv()
        handed[1].wait_recv()

    @pl.loop(groups, groups + (groups - 1) * paired)
    def _(g):
        start(step1(g))

    @pl.loop(0, first)
    def _(g):
        arrive(step1(g))
        start(step2(g))

    def row_steps(g):
        arrive(step2(g))
        start(step3(g))
        start(share(g, 0))

    @pl.loop(0, 2 * works + gives)
    def _(g):
        row_steps(g)

    def finish(g):
        arrive(step4(g))
        start(share(g, 3))
        for which in range(4):
            arrive(share(g, which))

    @pl.loop(0, blocks + 1)
    def _(i):
        @pl.when(i < blocks)
        def _():
            arrive(step3(i))
            start(step4(i))
            start(share(i, 1))
            start(share(i, 2))

            @pl.when(i + 2 < blocks)
            def _():
                row_steps(i + 2)

            @pl.when(i + groups < blocks)
            def _():
                arrive(step1(i + groups))
                start(step2(i + groups))

        @pl.when(i > 0)
        def _():
            g = i - 1
            finish(g)

            @pl.when((z == 0) & (g == 0))
            def _():
                take(0)
                norm(0, 0)

            @pl.when(z == 0)
            def _():
                project_kv(0, 0, g)
                project_q(0, g)
                attend(0, 0, (g,))

    share_y = pl.ds(2 * c, 2)
    whole = send(
        wv.at[0, share_y], wv.at[2 * groups - 1, share_y], ws.at[2], wr.at[2], up(1, r)
    )
    half_whole = same(wv.at[2 * groups - 1, share_y], ws.at[3], wr.at[3], sibling)

    @pl.when(gives == 1)
    def _():
        whole.start()

    @pl.when(paired == 1)
    def _():
        whole.wait_recv()
        half_whole.start()
        half_whole.wait_recv()

    @pl.loop(1 - (z + last_z) // (last_z + 1), chunks * works)
    def _(q):
        take(q)

        @pl.loop(0, 1 + paired)
        def _(k):
            layer(paired - k, q)

    @pl.when(z < last_z)
    def _():
        @pl.loop(0, chunks)
        def _(q):
            @pl.loop(0, groups)
            def _(g):
                @pl.when(gives == 1)
                def _():
                    hand_back(q, g).wait_recv()

                deliver(q, g)

    @pl.loop(0, blocks)
    def _(g):
        sent(step1(g))
        sent(step2(g))
        sent(step3(g))
        sent(step4(g))
        for which in range(4):
            sent(share(g, which))

    @pl.when(gives == 1)
    def _():
        sent(handed)
        whole.wait_send()

    @pl.when(paired == 1)
    def _():
        half_whole.wait_send()

    @pl.loop(0, chunks)
    def _(q):
        @pl.loop(0, groups)
        def _(g):
            @pl.when(r < ranks - 1)
            def _():
                @pl.loop(0, works + paired)
                def _(s):
                    halo_copy(s * chunks + q, g).wait_send()

                pass_copy(q, g).wait_send()

            @pl.when(paired == 1)
            def _():
                hand_back(q, g).wait_send()

            @pl.when((works == 1) & (z < last_z))
            def _():
                relay(q, g).wait_send()

            keep_copy(q, g).wait()

            @pl.when(r > 0)
            def _():
                pass_copy(q, g).wait_recv()

    @pl.when(r == 0)
    def _():
        first = out.at[0, :, pl.ds(0, rows)]
        pltpu.make_async_copy(first, first, cleared.at[0]).wait()


def shards(inputs, norm_gain, qkv_weight, batch_lengths, doc_lengths, doc_shift):
    chunks, rows, width = inputs.shape
    groups = KVHEADS
    there = pl.BlockSpec(memory_space=pl.ANY)
    dma = pltpu.SemaphoreType.DMA
    state = pltpu.VMEM((chunks, groups, rows, WIDE), BF)
    flags = pltpu.VMEM((chunks, rows, HEAD), F32)
    ring = dma((2, 2 * groups, 2))
    piece, tasks = dma((chunks, groups)), dma((2 * chunks, groups))
    return pl.pallas_call(
        kernel,
        out_shape=jax.ShapeDtypeStruct((1, chunks, 2 * rows, width), BF),
        in_specs=[there] * 6,
        out_specs=there,
        scratch_shapes=[
            pltpu.VMEM((2,) + norm_gain.shape, F32),
            pltpu.VMEM(doc_lengths.shape, jnp.int32),
            pltpu.VMEM(doc_shift.shape, jnp.int32),
            pltpu.SMEM(batch_lengths.shape, jnp.int32),
            dma((groups + 4,)),
            pltpu.VMEM((2 * groups, NY, NX, 2, 2, 32, COLS), BF),
            state,
            pltpu.VMEM((rows, width), BF),
            state,
            state,
            state,
            pltpu.VMEM((2 * chunks, groups, rows, 2 * HEAD), BF),
            pltpu.VMEM((2 * chunks, groups, 1, rows, 2 * HEAD), BF),
            pltpu.VMEM((groups, rows, WIDE), BF),
            pltpu.VMEM((chunks, 2, rows // 2, rows + rows // 2), F32),
            flags,
            flags,
            flags,
            pltpu.VMEM((rows, WIDE), BF),
            ring, ring, ring, ring, ring, ring, ring, ring,
            dma((2, 2 * groups, 4)), dma((2, 2 * groups, 4)),
            tasks, tasks, piece, piece, piece, piece, piece, piece,
            dma((4,)), dma((4,)), dma((1,)),
        ],
        compiler_params=pltpu.CompilerParams(
            collective_id=0, has_side_effects=True, vmem_limit_bytes=48 << 20
        ),
        name="relay",
    )(inputs, norm_gain, qkv_weight, doc_lengths, doc_shift, batch_lengths)


def solution(mesh):
    placed = (P(None, "cp", None), P("section", None), P("section", "cp", None), P(), P(), P())
    return jax.shard_map(
        shards,
        mesh=mesh,
        in_specs=placed,
        out_specs=P("section", None, "cp", None),
        check_vma=False,
    )
```

```python
import functools
import math

import jax
import jax.numpy as jnp
from jax import lax
from jax.experimental import pallas as pl
from jax.experimental.pallas import tpu as pltpu
from jax.sharding import PartitionSpec as P

MESH = pl.DeviceIdType.MESH
KVHEADS = 4
HEAD = 128
GROUP = 4
WIDE = GROUP * HEAD
COLS = WIDE + 2 * HEAD
NX, NY = 4, 4
EPSILON = 1e-05
NEGATIVE = -1e30
BF, F32 = jnp.bfloat16, jnp.float32
STEP = 1


def kernel(
    inp, gain_in, w, lens_in, shifts_in, blen_in, out,
    gain, lens, shifts, blen, fetched, wv, xin, xn, raw, keep, pass_on, kv, halo, qs,
    allow, live, sel_a, sel_b, zero,
    s1s, s1r, s2s, s2r, s3s, s3r, s4s, s4r, ds, dr,
    hs, hr, zs, zr, as_, ar, bs, br, ws, wr, cleared,
):
    z, r = lax.axis_index("section"), lax.axis_index("cp")
    last_z = lax.axis_size("section") - 1
    ranks = lax.axis_size("cp")
    c = r % 2
    x, y = (r // 2) % NX, r // (2 * NX)
    chunks, groups, rows = xin.shape[0], xin.shape[1], xin.shape[2]
    width = groups * WIDE
    back, half = rows, rows // 2

    def at(dx, dy):
        return (z, (((y + dy) % NY) * NX + (x + dx) % NX) * 2 + c)

    sibling = (z, r + 1 - 2 * c)
    right, left = (r + 1) % ranks, (r + ranks - 1) % ranks

    odd = z % 2
    paired = odd * ((z + last_z - 2) // (last_z + 1))
    gives = (1 - odd) * ((z + last_z - 1) // (last_z + 1))
    works = 1 - gives
    blocks = groups * works + (groups - 1) * paired + gives

    def up(k, rank):
        return ((z + k + last_z + 1) % (last_z + 1), rank)

    following = up(1 + (z + last_z) // (last_z + 1), r)

    barrier = pltpu.get_barrier_semaphore()
    peers = [sibling, at(1, 0), at(3, 0), at(0, 1), at(0, 3), (z, right), (z, left)]
    peers += [up(1, r), up(-1, r), up(2, r), up(-2, r)]
    for peer in peers:
        pl.semaphore_signal(barrier, inc=1, device_id=peer, device_id_type=MESH)

    def slot(s, g):
        return s * groups + (g + s * (groups - 1)) % groups

    for g in range(groups):
        spans = (
            (0, g * WIDE, WIDE),
            (WIDE, width + g * HEAD, HEAD),
            (WIDE + HEAD, width + (groups + g) * HEAD, HEAD),
        )
        for f in range(2):
            for to, first, count in spans:
                pltpu.make_async_copy(
                    w.at[0, pl.ds(32 * f, 32), pl.ds(first, count)],
                    wv.at[slot(0, g), y, x, c, f, :, pl.ds(to, count)],
                    fetched.at[g],
                ).start()
    small = [
        pltpu.make_async_copy(src, dst, fetched.at[groups + i])
        for i, (src, dst) in enumerate(
            ((lens_in, lens), (shifts_in, shifts), (blen_in, blen), (gain_in, gain.at[0]))
        )
    ]
    for copy in small:
        copy.start()

    @pl.when(z == 0)
    def _():
        for q in range(chunks):
            for g in range(groups):
                pltpu.make_async_copy(
                    inp.at[q, :, pl.ds(g * WIDE, WIDE)], xin.at[q, g], zr.at[q, g]
                ).start()

    mine = wv.at[pl.ds(1, groups - 1), y, x, c]
    for g in range(groups):
        block = wv.at[slot(0, g), y, x, c]
        pltpu.make_async_copy(block, block, fetched.at[g]).wait()
    pl.semaphore_wait(barrier, len(peers))

    def send(src, dst, ss, rs, to):
        return pltpu.make_async_remote_copy(
            src_ref=src, dst_ref=dst, send_sem=ss, recv_sem=rs, device_id=to, device_id_type=MESH
        )

    def same(ref, ss, rs, to):
        return send(ref, ref, ss, rs, to)

    x1, x3, y1, y3 = (x + 1) % NX, (x + 3) % NX, (y + 1) % NY, (y + 3) % NY
    x2, y2 = (x + 2) % NX, (y + 2) % NY
    low, high = pl.ds(0, 16), pl.ds(16, 16)

    def step1(g):
        return [
            same(wv.at[g, y, x, c, 0], s1s.at[0, g, 0], s1r.at[0, g, 0], at(1, 0)),
            same(wv.at[g, y, x, c, 0], s1s.at[0, g, 1], s1r.at[0, g, 1], at(3, 0)),
            same(wv.at[g, y, x, c, 1], s1s.at[1, g, 0], s1r.at[1, g, 0], at(0, 1)),
            same(wv.at[g, y, x, c, 1], s1s.at[1, g, 1], s1r.at[1, g, 1], at(0, 3)),
        ]

    def step2(g):
        return [
            same(wv.at[g, y, x3, c, 0, low], s2s.at[0, g, 0], s2r.at[0, g, 0], at(1, 0)),
            same(wv.at[g, y, x1, c, 0, high], s2s.at[0, g, 1], s2r.at[0, g, 1], at(3, 0)),
            same(wv.at[g, y3, x, c, 1, low], s2s.at[1, g, 0], s2r.at[1, g, 0], at(0, 1)),
            same(wv.at[g, y1, x, c, 1, high], s2s.at[1, g, 1], s2r.at[1, g, 1], at(0, 3)),
        ]

    def step3(g):
        return [
            same(wv.at[g, y, :, c, 0], s3s.at[0, g, 0], s3r.at[0, g, 0], at(0, 1)),
            same(wv.at[g, y, :, c, 0], s3s.at[0, g, 1], s3r.at[0, g, 1], at(0, 3)),
            same(wv.at[g, :, x, c, 1], s3s.at[1, g, 0], s3r.at[1, g, 0], at(1, 0)),
            same(wv.at[g, :, x, c, 1], s3s.at[1, g, 1], s3r.at[1, g, 1], at(3, 0)),
        ]

    def step4(g):
        return [
            same(wv.at[g, y3, :, c, 0, low], s4s.at[0, g, 0], s4r.at[0, g, 0], at(0, 1)),
            same(wv.at[g, y1, :, c, 0, high], s4s.at[0, g, 1], s4r.at[0, g, 1], at(0, 3)),
            same(wv.at[g, :, x3, c, 1, low], s4s.at[1, g, 0], s4r.at[1, g, 0], at(1, 0)),
            same(wv.at[g, :, x1, c, 1, high], s4s.at[1, g, 1], s4r.at[1, g, 1], at(3, 0)),
        ]

    def share(g, which):
        row, col = ((y, x), (y3, x3), (y1, x1), (y2, x2))[which]
        return [
            same(wv.at[g, row, :, c, 0], ds.at[0, g, which], dr.at[0, g, which], sibling),
            same(wv.at[g, :, col, c, 1], ds.at[1, g, which], dr.at[1, g, which], sibling),
        ]

    def start(copies):
        for copy in copies:
            copy.start()

    def arrive(copies):
        for copy in copies:
            copy.wait_recv()

    def sent(copies):
        for copy in copies:
            copy.wait_send()

    first = works * groups + gives

    @pl.loop(0, first)
    def _(g):
        start(step1(g))

    handed = [
        send(mine, wv.at[pl.ds(groups, groups - 1), y, x, c], ws.at[0], wr.at[0], up(1, r)),
        send(gain.at[0], gain.at[1], ws.at[1], wr.at[1], up(1, r)),
    ]

    @pl.when(gives == 1)
    def _():
        handed[0].start()

    for copy in small:
        copy.wait()

    @pl.when(gives == 1)
    def _():
        handed[1].start()

    @pl.when((r == 0) & (works == 1))
    def _():
        halo[...] = jnp.zeros_like(halo)

    def columns(g):
        return pl.ds(pl.multiple_of(g * WIDE, WIDE), WIDE)

    def blank(q, g):
        return pltpu.make_async_copy(
            zero, out.at[0, q, pl.ds(0, rows), columns(g)], cleared.at[0]
        )

    def norm(s, q):
        gains = gain[s]


        @pl.loop(0, rows // half)
        def _(i):
            part = pl.ds(pl.multiple_of(i * half, half), half)
            values = [xin[q, g, part].astype(F32) for g in range(groups)]
            total = sum(jnp.sum(v * v, axis=1, keepdims=True) for v in values)
            inverse = lax.rsqrt(total * (1.0 / width) + EPSILON)
            for g in range(groups):
                cols = slice(g * WIDE, (g + 1) * WIDE)
                xn[part, cols] = (values[g] * inverse * gains[:, cols]).astype(BF)

    def halo_copy(t, g):
        return send(kv.at[t, g], halo.at[t, g, 0], hs.at[t, g], hr.at[t, g], (z, right))

    def relay(q, g):
        return send(xin.at[q, g], xin.at[q, g], zs.at[q, g], zr.at[q, g], following)

    def hand_back(q, g):
        return send(raw.at[q, g], xin.at[q, g], as_.at[q, g], zr.at[q, g], up(-1, r))

    def keep_copy(q, g):
        return pltpu.make_async_copy(
            keep.at[q, g], out.at[0, q, pl.ds(rows, rows), columns(g)], ar.at[q, g]
        )

    def pass_copy(q, g):
        return send(
            pass_on.at[q, g], out.at[0, q, pl.ds(0, rows), columns(g)],
            bs.at[q, g], br.at[q, g], (z, right),
        )

    def deliver(q, g):
        for h in range(GROUP):
            cols = slice(h * HEAD, (h + 1) * HEAD)
            result = xin[q, g, :, cols]
            keep[q, g, :, cols] = jnp.where(sel_a[q] > 0.5, result, 0.0).astype(BF)
            pass_on[q, g, :, cols] = jnp.where(sel_b[q] > 0.5, result, 0.0).astype(BF)
        keep_copy(q, g).start()

        @pl.when(r < ranks - 1)
        def _():
            pass_copy(q, g).start()

    def weights(s, g, first, count):
        block = wv[slot(s, g), :, :, :, :, :, first : first + count]
        return block.reshape(width, count)

    def project_kv(s, q, g):
        t = s * chunks + q
        kv[t, g] = jnp.dot(
            xn[...], weights(s, g, WIDE, 2 * HEAD), preferred_element_type=F32
        ).astype(BF)

        @pl.when(r < ranks - 1)
        def _():
            halo_copy(t, g).start()

    def project_q(s, g):
        qs[g] = jnp.dot(xn[...], weights(s, g, 0, WIDE), preferred_element_type=F32).astype(BF)

    heads = [slice(h * HEAD, (h + 1) * HEAD) for h in range(GROUP)]
    parts = [slice(i * half, (i + 1) * half) for i in range(2)]

    def attend(s, q, some):
        t = s * chunks + q
        for g in some:

            @pl.when(r > 0)
            def _():
                halo_copy(t, g).wait_recv()

        def seen_rows(g, i, cols):
            earlier, own = halo[t, g, 0, i * half :, cols], kv[t, g, : (i + 1) * half, cols]
            return jnp.concatenate([earlier, own], axis=0)

        tiles = [(g, i) for g in some for i in range(2)]
        seen = [jnp.concatenate([allow[q, i] > 0.5] * GROUP, axis=0) for i in range(2)]
        ones = jnp.ones((back + half, HEAD), BF)
        scores = [
            lax.dot_general(
                jnp.concatenate([qs[g, parts[i], cols] for cols in heads], axis=0),
                seen_rows(g, i, heads[0]),
                (((1,), (1,)), ((), ())),
                preferred_element_type=F32,
            )
            for g, i in tiles
        ]
        scores = [jnp.where(seen[i], a, NEGATIVE) for (_, i), a in zip(tiles, scores)]
        highest = [jnp.max(a, axis=1, keepdims=True) for a in scores]
        scale = math.log2(math.e) / math.sqrt(HEAD)
        weighted = [jnp.exp2((a - m) * scale).astype(BF) for a, m in zip(scores, highest)]
        mixed = [
            jnp.dot(
                e, jnp.concatenate([seen_rows(g, i, heads[1]), ones], axis=1),
                preferred_element_type=F32,
            )
            for (g, i), e in zip(tiles, weighted)
        ]
        for (g, i), mix in zip(tiles, mixed):
            mix = mix[:, :HEAD] / mix[:, HEAD:]
            alive = live[q, parts[i]] > 0.5
            for h, cols in enumerate(heads):
                more = mix[h * half : (h + 1) * half]
                result = jnp.where(alive, xin[q, g, parts[i], cols].astype(F32) + more, 0.0)
                xin[q, g, parts[i], cols] = result.astype(BF)

        for g in some:
            send_on(s, q, g)

    def send_on(s, q, g):
        @pl.when((s == 0) & (z < last_z))
        def _():
            relay(q, g).start()

        @pl.when(s == 1)
        def _():
            raw[q, g] = xin[q, g]
            hand_back(q, g).start()

        @pl.when((s == 0) & (z == last_z))
        def _():
            deliver(q, g)

    def take(q):
        @pl.loop(0, groups)
        def _(g):
            relay(q, g).wait_recv()

    def layer(s, q):
        norm(s, q)
        for g in range(groups):
            project_kv(s, q, g)
        for g in range(groups):
            project_q(s, g)

        @pl.loop(0, groups // STEP)
        def _(g):
            attend(s, q, tuple(g * STEP + i for i in range(STEP)))

    @pl.when(paired == 1)
    def _():
        handed[0].wait_recv()
        handed[1].wait_recv()

    @pl.loop(groups, groups + (groups - 1) * paired)
    def _(g):
        start(step1(g))

    @pl.loop(0, first)
    def _(g):
        arrive(step1(g))
        start(step2(g))

    def row_steps(g):
        arrive(step2(g))
        start(step3(g))

        @pl.when(works == 1)
        def _():
            start(share(g, 0))


    @pl.loop(0, 2 * works + gives)
    def _(g):
        row_steps(g)

    spot = lax.broadcasted_iota(jnp.int32, (HEAD, HEAD), 0)
    until = lax.broadcasted_iota(jnp.int32, (HEAD, HEAD), 1)
    upto = jnp.where(spot <= until, 1.0, 0.0).astype(BF)
    length = lens[...].astype(F32)
    ends = jnp.dot(length.astype(BF), upto, preferred_element_type=F32)
    starts = ends - length
    moves = shifts[...].astype(F32)
    base = (r * rows).astype(F32)
    for q in range(chunks):
        begin, end, move = starts[q : q + 1], ends[q : q + 1], moves[q : q + 1]
        place = lax.broadcasted_iota(jnp.int32, (rows, HEAD), 0).astype(F32) + base
        before, after = begin <= place, end > place
        doc_start = jnp.max(jnp.where(before, begin, -1.0), axis=1, keepdims=True)
        doc_end = jnp.min(jnp.where(after, end, 1e9), axis=1, keepdims=True)
        shift = jnp.max(jnp.where(before & after, move, 0.0), axis=1, keepdims=True)
        edge = base + rows
        moved = (doc_start >= base) & (shift > 0.5) & (edge < float(rows) * ranks)
        to_next = jnp.where((doc_end > edge) | moved, 1.0, 0.0)
        alive = jnp.where(place < blen[q].astype(F32), 1.0, 0.0)
        live[q] = alive
        sel_a[q] = alive * (1.0 - to_next)
        sel_b[q] = alive * to_next
        for i in range(2):
            part = slice(i * half, (i + 1) * half)
            span = (half, back + half)
            query = lax.broadcasted_iota(jnp.int32, span, 0).astype(F32) + (base + i * half)
            key = lax.broadcasted_iota(jnp.int32, span, 1).astype(F32) + (base + i * half - back)
            seen = (key >= doc_start[part]) & (key <= query)
            allow[q, i] = jnp.where(seen, 1.0, 0.0)

    def finish(g):
        arrive(step4(g))

        @pl.when(works == 1)
        def _():
            start(share(g, 3))
            for which in range(4):
                arrive(share(g, which))


    @pl.loop(0, blocks + 2 - (z + last_z) // (last_z + 1))
    def _(i):
        @pl.when(i < blocks)
        def _():
            arrive(step3(i))
            start(step4(i))

            @pl.when(works == 1)
            def _():
                start(share(i, 1))
                start(share(i, 2))


            @pl.when(i + 2 < blocks)
            def _():
                row_steps(i + 2)

            @pl.when(i + groups < blocks)
            def _():
                arrive(step1(i + groups))
                start(step2(i + groups))

        @pl.when((z == 0) & (i > 1))
        def _():
            attend(0, 0, (i - 2,))

        @pl.when((i > 0) & (i <= blocks))
        def _():
            g = i - 1
            finish(g)

            @pl.when((z == 0) & (g == 0))
            def _():
                take(0)
                norm(0, 0)

            @pl.when(z == 0)
            def _():
                project_kv(0, 0, g)
                project_q(0, g)

    whole = send(
        wv.at[0, :, :, c], wv.at[2 * groups - 1, :, :, c], ws.at[2], wr.at[2], up(1, r)
    )
    half_whole = same(wv.at[2 * groups - 1, :, :, c], ws.at[3], wr.at[3], sibling)

    @pl.when(gives == 1)
    def _():
        whole.start()

    @pl.when(paired == 1)
    def _():
        whole.wait_recv()
        half_whole.start()
        half_whole.wait_recv()

    @pl.loop(1 - (z + last_z) // (last_z + 1), chunks * works)
    def _(q):
        take(q)

        @pl.loop(0, 1 + paired)
        def _(k):
            layer(paired - k, q)

    @pl.when(r == 0)
    def _():
        zero[...] = jnp.zeros_like(zero)

        @pl.loop(0, chunks)
        def _(q):
            @pl.loop(0, groups)
            def _(g):
                blank(q, g).start()

    @pl.when(z < last_z)
    def _():
        @pl.loop(0, chunks)
        def _(q):
            @pl.loop(0, groups)
            def _(g):
                @pl.when(gives == 1)
                def _():
                    hand_back(q, g).wait_recv()

                deliver(q, g)

    @pl.loop(0, blocks)
    def _(g):
        sent(step1(g))
        sent(step2(g))
        sent(step3(g))
        sent(step4(g))

        @pl.when(works == 1)
        def _():
            for which in range(4):
                sent(share(g, which))


    @pl.when(gives == 1)
    def _():
        sent(handed)
        whole.wait_send()

    @pl.when(paired == 1)
    def _():
        half_whole.wait_send()

    @pl.loop(0, chunks)
    def _(q):
        @pl.loop(0, groups)
        def _(g):
            @pl.when(r < ranks - 1)
            def _():
                @pl.loop(0, works + paired)
                def _(s):
                    halo_copy(s * chunks + q, g).wait_send()

                pass_copy(q, g).wait_send()

            @pl.when(paired == 1)
            def _():
                hand_back(q, g).wait_send()

            @pl.when((works == 1) & (z < last_z))
            def _():
                relay(q, g).wait_send()

            keep_copy(q, g).wait()

            @pl.when(r > 0)
            def _():
                pass_copy(q, g).wait_recv()

    @pl.when(r == 0)
    def _():
        first = out.at[0, :, pl.ds(0, rows)]
        pltpu.make_async_copy(first, first, cleared.at[0]).wait()


def shards(inputs, norm_gain, qkv_weight, batch_lengths, doc_lengths, doc_shift):
    chunks, rows, width = inputs.shape
    groups = KVHEADS
    there = pl.BlockSpec(memory_space=pl.ANY)
    dma = pltpu.SemaphoreType.DMA
    state = pltpu.VMEM((chunks, groups, rows, WIDE), BF)
    flags = pltpu.VMEM((chunks, rows, HEAD), F32)
    ring = dma((2, 2 * groups, 2))
    piece, tasks = dma((chunks, groups)), dma((2 * chunks, groups))
    return pl.pallas_call(
        kernel,
        out_shape=jax.ShapeDtypeStruct((1, chunks, 2 * rows, width), BF),
        in_specs=[there] * 6,
        out_specs=there,
        scratch_shapes=[
            pltpu.VMEM((2,) + norm_gain.shape, F32),
            pltpu.VMEM(doc_lengths.shape, jnp.int32),
            pltpu.VMEM(doc_shift.shape, jnp.int32),
            pltpu.SMEM(batch_lengths.shape, jnp.int32),
            dma((groups + 4,)),
            pltpu.VMEM((2 * groups, NY, NX, 2, 2, 32, COLS), BF),
            state,
            pltpu.VMEM((rows, width), BF),
            state,
            state,
            state,
            pltpu.VMEM((2 * chunks, groups, rows, 2 * HEAD), BF),
            pltpu.VMEM((2 * chunks, groups, 1, rows, 2 * HEAD), BF),
            pltpu.VMEM((groups, rows, WIDE), BF),
            pltpu.VMEM((chunks, 2, rows // 2, rows + rows // 2), F32),
            flags,
            flags,
            flags,
            pltpu.VMEM((rows, WIDE), BF),
            ring, ring, ring, ring, ring, ring, ring, ring,
            dma((2, 2 * groups, 4)), dma((2, 2 * groups, 4)),
            tasks, tasks, piece, piece, piece, piece, piece, piece,
            dma((4,)), dma((4,)), dma((1,)),
        ],
        compiler_params=pltpu.CompilerParams(
            collective_id=0, has_side_effects=True, vmem_limit_bytes=48 << 20
        ),
        name="relay",
    )(inputs, norm_gain, qkv_weight, doc_lengths, doc_shift, batch_lengths)


def solution(mesh):
    placed = (P(None, "cp", None), P("section", None), P("section", "cp", None), P(), P(), P())
    return jax.shard_map(
        shards,
        mesh=mesh,
        in_specs=placed,
        out_specs=P("section", None, "cp", None),
        check_vma=False,
    )
```

```python
import functools
import math

import jax
import jax.numpy as jnp
from jax import lax
from jax.experimental import pallas as pl
from jax.experimental.pallas import tpu as pltpu
from jax.sharding import PartitionSpec as P

MESH = pl.DeviceIdType.MESH
KVHEADS = 4
HEAD = 128
GROUP = 4
WIDE = GROUP * HEAD
COLS = WIDE + 2 * HEAD
NX, NY = 4, 4
EPSILON = 1e-05
NEGATIVE = -1e30
BF, F32 = jnp.bfloat16, jnp.float32
STEP = 1


def kernel(
    inp, gain_in, w, lens_in, shifts_in, blen_in, out,
    gain, lens, shifts, blen, fetched, wv, xin, xn, raw, keep, pass_on, kv, halo, qs,
    allow, live, sel_a, sel_b, zero,
    s1s, s1r, s2s, s2r, s3s, s3r, s4s, s4r, ds, dr,
    hs, hr, zs, zr, as_, ar, bs, br, ws, wr, cleared,
):
    z, r = lax.axis_index("section"), lax.axis_index("cp")
    last_z = lax.axis_size("section") - 1
    ranks = lax.axis_size("cp")
    c = r % 2
    x, y = (r // 2) % NX, r // (2 * NX)
    chunks, groups, rows = xin.shape[0], xin.shape[1], xin.shape[2]
    width = groups * WIDE
    back, half = rows, rows // 2

    def at(dx, dy):
        return (z, (((y + dy) % NY) * NX + (x + dx) % NX) * 2 + c)

    sibling = (z, r + 1 - 2 * c)
    right, left = (r + 1) % ranks, (r + ranks - 1) % ranks

    odd = z % 2
    paired = odd * ((z + last_z - 2) // (last_z + 1))
    gives = (1 - odd) * ((z + last_z - 1) // (last_z + 1))
    works = 1 - gives
    blocks = groups * works + (groups - 1) * paired + gives

    def up(k, rank):
        return ((z + k + last_z + 1) % (last_z + 1), rank)

    following = up(1 + (z + last_z) // (last_z + 1), r)

    barrier = pltpu.get_barrier_semaphore()
    peers = [sibling, at(1, 0), at(3, 0), at(0, 1), at(0, 3), (z, right), (z, left)]
    peers += [up(1, r), up(-1, r), up(2, r), up(-2, r)]
    for peer in peers:
        pl.semaphore_signal(barrier, inc=1, device_id=peer, device_id_type=MESH)

    def slot(s, g):
        return s * groups + (g + s * (groups - 1)) % groups

    for g in range(groups):
        spans = (
            (0, g * WIDE, WIDE),
            (WIDE, width + g * HEAD, HEAD),
            (WIDE + HEAD, width + (groups + g) * HEAD, HEAD),
        )
        for f in range(2):
            for to, first, count in spans:
                pltpu.make_async_copy(
                    w.at[0, pl.ds(32 * f, 32), pl.ds(first, count)],
                    wv.at[slot(0, g), y, x, c, f, :, pl.ds(to, count)],
                    fetched.at[g],
                ).start()
    small = [
        pltpu.make_async_copy(src, dst, fetched.at[groups + i])
        for i, (src, dst) in enumerate(
            ((lens_in, lens), (shifts_in, shifts), (blen_in, blen), (gain_in, gain.at[0]))
        )
    ]
    for copy in small:
        copy.start()

    @pl.when(z == 0)
    def _():
        for q in range(chunks):
            for g in range(groups):
                pltpu.make_async_copy(
                    inp.at[q, :, pl.ds(g * WIDE, WIDE)], xin.at[q, g], zr.at[q, g]
                ).start()

    mine = wv.at[pl.ds(1, groups - 1), y, x, c]
    for g in range(groups):
        block = wv.at[slot(0, g), y, x, c]
        pltpu.make_async_copy(block, block, fetched.at[g]).wait()
    pl.semaphore_wait(barrier, len(peers))

    def send(src, dst, ss, rs, to):
        return pltpu.make_async_remote_copy(
            src_ref=src, dst_ref=dst, send_sem=ss, recv_sem=rs, device_id=to, device_id_type=MESH
        )

    def same(ref, ss, rs, to):
        return send(ref, ref, ss, rs, to)

    x1, x3, y1, y3 = (x + 1) % NX, (x + 3) % NX, (y + 1) % NY, (y + 3) % NY
    x2, y2 = (x + 2) % NX, (y + 2) % NY
    low, high = pl.ds(0, 16), pl.ds(16, 16)

    def step1(g):
        return [
            same(wv.at[g, y, x, c, 0], s1s.at[0, g, 0], s1r.at[0, g, 0], at(1, 0)),
            same(wv.at[g, y, x, c, 0], s1s.at[0, g, 1], s1r.at[0, g, 1], at(3, 0)),
            same(wv.at[g, y, x, c, 1], s1s.at[1, g, 0], s1r.at[1, g, 0], at(0, 1)),
            same(wv.at[g, y, x, c, 1], s1s.at[1, g, 1], s1r.at[1, g, 1], at(0, 3)),
        ]

    def step2(g):
        return [
            same(wv.at[g, y, x3, c, 0, low], s2s.at[0, g, 0], s2r.at[0, g, 0], at(1, 0)),
            same(wv.at[g, y, x1, c, 0, high], s2s.at[0, g, 1], s2r.at[0, g, 1], at(3, 0)),
            same(wv.at[g, y3, x, c, 1, low], s2s.at[1, g, 0], s2r.at[1, g, 0], at(0, 1)),
            same(wv.at[g, y1, x, c, 1, high], s2s.at[1, g, 1], s2r.at[1, g, 1], at(0, 3)),
        ]

    def step3(g):
        return [
            same(wv.at[g, y, :, c, 0], s3s.at[0, g, 0], s3r.at[0, g, 0], at(0, 1)),
            same(wv.at[g, y, :, c, 0], s3s.at[0, g, 1], s3r.at[0, g, 1], at(0, 3)),
            same(wv.at[g, :, x, c, 1], s3s.at[1, g, 0], s3r.at[1, g, 0], at(1, 0)),
            same(wv.at[g, :, x, c, 1], s3s.at[1, g, 1], s3r.at[1, g, 1], at(3, 0)),
        ]

    def step4(g):
        return [
            same(wv.at[g, y3, :, c, 0, low], s4s.at[0, g, 0], s4r.at[0, g, 0], at(0, 1)),
            same(wv.at[g, y1, :, c, 0, high], s4s.at[0, g, 1], s4r.at[0, g, 1], at(0, 3)),
            same(wv.at[g, :, x3, c, 1, low], s4s.at[1, g, 0], s4r.at[1, g, 0], at(1, 0)),
            same(wv.at[g, :, x1, c, 1, high], s4s.at[1, g, 1], s4r.at[1, g, 1], at(3, 0)),
        ]

    def share(g, which):
        row, col = ((y, x), (y3, x3), (y1, x1), (y2, x2))[which]
        return [
            same(wv.at[g, row, :, c, 0], ds.at[0, g, which], dr.at[0, g, which], sibling),
            same(wv.at[g, :, col, c, 1], ds.at[1, g, which], dr.at[1, g, which], sibling),
        ]

    def start(copies):
        for copy in copies:
            copy.start()

    def arrive(copies):
        for copy in copies:
            copy.wait_recv()

    def sent(copies):
        for copy in copies:
            copy.wait_send()

    first = works * groups + gives

    @pl.loop(0, first)
    def _(g):
        start(step1(g))

    handed = [
        send(mine, wv.at[pl.ds(groups, groups - 1), y, x, c], ws.at[0], wr.at[0], up(1, r)),
        send(gain.at[0], gain.at[1], ws.at[1], wr.at[1], up(1, r)),
    ]

    @pl.when(gives == 1)
    def _():
        handed[0].start()

    for copy in small:
        copy.wait()

    @pl.when(gives == 1)
    def _():
        handed[1].start()

    @pl.when((r == 0) & (works == 1))
    def _():
        halo[...] = jnp.zeros_like(halo)

    def columns(g):
        return pl.ds(pl.multiple_of(g * WIDE, WIDE), WIDE)

    def blank(q, g):
        return pltpu.make_async_copy(
            zero, out.at[0, q, pl.ds(0, rows), columns(g)], cleared.at[0]
        )

    def norm(s, q):
        gains = gain[s]


        @pl.loop(0, rows // half)
        def _(i):
            part = pl.ds(pl.multiple_of(i * half, half), half)
            values = [xin[q, g, part].astype(F32) for g in range(groups)]
            total = sum(jnp.sum(v * v, axis=1, keepdims=True) for v in values)
            inverse = lax.rsqrt(total * (1.0 / width) + EPSILON)
            for g in range(groups):
                cols = slice(g * WIDE, (g + 1) * WIDE)
                xn[q, part, cols] = (values[g] * inverse * gains[:, cols]).astype(BF)

    def halo_copy(t, g):
        return send(kv.at[t, g], halo.at[t, g, 0], hs.at[t, g], hr.at[t, g], (z, right))

    def relay(q, g):
        return send(xin.at[q, g], xin.at[q, g], zs.at[q, g], zr.at[q, g], following)

    def hand_back(q, g):
        return send(raw.at[q, g], xin.at[q, g], as_.at[q, g], zr.at[q, g], up(-1, r))

    def keep_copy(q, g):
        return pltpu.make_async_copy(
            keep.at[q, g], out.at[0, q, pl.ds(rows, rows), columns(g)], ar.at[q, g]
        )

    def pass_copy(q, g):
        return send(
            pass_on.at[q, g], out.at[0, q, pl.ds(0, rows), columns(g)],
            bs.at[q, g], br.at[q, g], (z, right),
        )

    def deliver(q, g):
        for h in range(GROUP):
            cols = slice(h * HEAD, (h + 1) * HEAD)
            result = xin[q, g, :, cols]
            keep[q, g, :, cols] = jnp.where(sel_a[q] > 0.5, result, 0.0).astype(BF)
            pass_on[q, g, :, cols] = jnp.where(sel_b[q] > 0.5, result, 0.0).astype(BF)
        keep_copy(q, g).start()

        @pl.when(r < ranks - 1)
        def _():
            pass_copy(q, g).start()

    def weights(s, g, first, count):
        block = wv[slot(s, g), :, :, :, :, :, first : first + count]
        return block.reshape(width, count)

    def project_kv(s, q, g, held=0):
        t = s * chunks + q
        kv[t, g] = jnp.dot(
            xn[q], weights(s, g, WIDE, 2 * HEAD), preferred_element_type=F32
        ).astype(BF)

        @pl.when((r < ranks - 1) & (held == 0))
        def _():
            halo_copy(t, g).start()

    def project_q(s, q, g):
        qs[g] = jnp.dot(xn[q], weights(s, g, 0, WIDE), preferred_element_type=F32).astype(BF)

    heads = [slice(h * HEAD, (h + 1) * HEAD) for h in range(GROUP)]
    parts = [slice(i * half, (i + 1) * half) for i in range(2)]

    def attend(s, q, some):
        t = s * chunks + q
        for g in some:

            @pl.when(r > 0)
            def _():
                halo_copy(t, g).wait_recv()

        def seen_rows(g, i, cols):
            earlier, own = halo[t, g, 0, i * half :, cols], kv[t, g, : (i + 1) * half, cols]
            return jnp.concatenate([earlier, own], axis=0)

        tiles = [(g, i) for g in some for i in range(2)]
        seen = [jnp.concatenate([allow[q, i] > 0.5] * GROUP, axis=0) for i in range(2)]
        ones = jnp.ones((back + half, HEAD), BF)
        scores = [
            lax.dot_general(
                jnp.concatenate([qs[g, parts[i], cols] for cols in heads], axis=0),
                seen_rows(g, i, heads[0]),
                (((1,), (1,)), ((), ())),
                preferred_element_type=F32,
            )
            for g, i in tiles
        ]
        scores = [jnp.where(seen[i], a, NEGATIVE) for (_, i), a in zip(tiles, scores)]
        highest = [jnp.max(a, axis=1, keepdims=True) for a in scores]
        scale = math.log2(math.e) / math.sqrt(HEAD)
        weighted = [jnp.exp2((a - m) * scale).astype(BF) for a, m in zip(scores, highest)]
        mixed = [
            jnp.dot(
                e, jnp.concatenate([seen_rows(g, i, heads[1]), ones], axis=1),
                preferred_element_type=F32,
            )
            for (g, i), e in zip(tiles, weighted)
        ]
        for (g, i), mix in zip(tiles, mixed):
            mix = mix[:, :HEAD] / mix[:, HEAD:]
            alive = live[q, parts[i]] > 0.5
            for h, cols in enumerate(heads):
                more = mix[h * half : (h + 1) * half]
                result = jnp.where(alive, xin[q, g, parts[i], cols].astype(F32) + more, 0.0)
                xin[q, g, parts[i], cols] = result.astype(BF)

        for g in some:
            send_on(s, q, g)

    def send_on(s, q, g):
        @pl.when((s == 0) & (z < last_z))
        def _():
            relay(q, g).start()

        @pl.when(s == 1)
        def _():
            raw[q, g] = xin[q, g]
            hand_back(q, g).start()

        @pl.when((s == 0) & (z == last_z))
        def _():
            deliver(q, g)

    def take(q):
        @pl.loop(0, groups)
        def _(g):
            relay(q, g).wait_recv()

    def layer(s, q):
        @pl.when(z > 0)
        def _():
            norm(s, q)
            for g in range(groups):
                project_kv(s, q, g)

        for g in range(groups):
            project_q(s, q, g)

        @pl.loop(0, groups // STEP)
        def _(g):
            attend(s, q, tuple(g * STEP + i for i in range(STEP)))

    @pl.when(paired == 1)
    def _():
        handed[0].wait_recv()
        handed[1].wait_recv()

    @pl.loop(groups, groups + (groups - 1) * paired)
    def _(g):
        start(step1(g))

    @pl.loop(0, first)
    def _(g):
        arrive(step1(g))
        start(step2(g))

    def row_steps(g):
        arrive(step2(g))
        start(step3(g))

        @pl.when(works == 1)
        def _():
            start(share(g, 0))


    @pl.loop(0, 2 * works + gives)
    def _(g):
        row_steps(g)

    spot = lax.broadcasted_iota(jnp.int32, (HEAD, HEAD), 0)
    until = lax.broadcasted_iota(jnp.int32, (HEAD, HEAD), 1)
    upto = jnp.where(spot <= until, 1.0, 0.0).astype(BF)
    length = lens[...].astype(F32)
    ends = jnp.dot(length.astype(BF), upto, preferred_element_type=F32)
    starts = ends - length
    moves = shifts[...].astype(F32)
    base = (r * rows).astype(F32)
    for q in range(chunks):
        begin, end, move = starts[q : q + 1], ends[q : q + 1], moves[q : q + 1]
        place = lax.broadcasted_iota(jnp.int32, (rows, HEAD), 0).astype(F32) + base
        before, after = begin <= place, end > place
        doc_start = jnp.max(jnp.where(before, begin, -1.0), axis=1, keepdims=True)
        doc_end = jnp.min(jnp.where(after, end, 1e9), axis=1, keepdims=True)
        shift = jnp.max(jnp.where(before & after, move, 0.0), axis=1, keepdims=True)
        edge = base + rows
        moved = (doc_start >= base) & (shift > 0.5) & (edge < float(rows) * ranks)
        to_next = jnp.where((doc_end > edge) | moved, 1.0, 0.0)
        alive = jnp.where(place < blen[q].astype(F32), 1.0, 0.0)
        live[q] = alive
        sel_a[q] = alive * (1.0 - to_next)
        sel_b[q] = alive * to_next
        for i in range(2):
            part = slice(i * half, (i + 1) * half)
            span = (half, back + half)
            query = lax.broadcasted_iota(jnp.int32, span, 0).astype(F32) + (base + i * half)
            key = lax.broadcasted_iota(jnp.int32, span, 1).astype(F32) + (base + i * half - back)
            seen = (key >= doc_start[part]) & (key <= query)
            allow[q, i] = jnp.where(seen, 1.0, 0.0)

    def finish(g):
        arrive(step4(g))

        @pl.when(works == 1)
        def _():
            start(share(g, 3))
            for which in range(4):
                arrive(share(g, which))


    @pl.loop(0, blocks + 2 - (z + last_z) // (last_z + 1))
    def _(i):
        @pl.when(i < blocks)
        def _():
            arrive(step3(i))
            start(step4(i))

            @pl.when(works == 1)
            def _():
                start(share(i, 1))
                start(share(i, 2))


            @pl.when(i + 2 < blocks)
            def _():
                row_steps(i + 2)

            @pl.when(i + groups < blocks)
            def _():
                arrive(step1(i + groups))
                start(step2(i + groups))

        @pl.when((z == 0) & (i > 1))
        def _():
            attend(0, 0, (i - 2,))

        @pl.when((i > 0) & (i <= blocks))
        def _():
            g = i - 1
            finish(g)

            @pl.when((z == 0) & (g == 0))
            def _():
                @pl.loop(0, chunks)
                def _(q):
                    take(q)
                    norm(0, q)

            @pl.when(z == 0)
            def _():
                project_kv(0, 0, g)
                project_q(0, 0, g)
                project_kv(0, 1, g, 1)

                @pl.when((g == groups - 1) & (r < ranks - 1))
                def _():
                    @pl.loop(0, groups)
                    def _(k):
                        halo_copy(1, k).start()

    whole = send(
        wv.at[0, :, :, c], wv.at[2 * groups - 1, :, :, c], ws.at[2], wr.at[2], up(1, r)
    )
    half_whole = same(wv.at[2 * groups - 1, :, :, c], ws.at[3], wr.at[3], sibling)

    @pl.when(gives == 1)
    def _():
        whole.start()

    @pl.when(paired == 1)
    def _():
        whole.wait_recv()
        half_whole.start()
        half_whole.wait_recv()

    @pl.loop(1 - (z + last_z) // (last_z + 1), chunks * works)
    def _(q):
        @pl.when(z > 0)
        def _():
            take(q)

        @pl.loop(0, 1 + paired)
        def _(k):
            layer(paired - k, q)

    @pl.when(r == 0)
    def _():
        zero[...] = jnp.zeros_like(zero)

        @pl.loop(0, chunks)
        def _(q):
            @pl.loop(0, groups)
            def _(g):
                blank(q, g).start()

    @pl.when(z < last_z)
    def _():
        @pl.loop(0, chunks)
        def _(q):
            @pl.loop(0, groups)
            def _(g):
                @pl.when(gives == 1)
                def _():
                    hand_back(q, g).wait_recv()

                deliver(q, g)

    @pl.loop(0, blocks)
    def _(g):
        sent(step1(g))
        sent(step2(g))
        sent(step3(g))
        sent(step4(g))

        @pl.when(works == 1)
        def _():
            for which in range(4):
                sent(share(g, which))


    @pl.when(gives == 1)
    def _():
        sent(handed)
        whole.wait_send()

    @pl.when(paired == 1)
    def _():
        half_whole.wait_send()

    @pl.loop(0, chunks)
    def _(q):
        @pl.loop(0, groups)
        def _(g):
            @pl.when(r < ranks - 1)
            def _():
                @pl.loop(0, works + paired)
                def _(s):
                    halo_copy(s * chunks + q, g).wait_send()

                pass_copy(q, g).wait_send()

            @pl.when(paired == 1)
            def _():
                hand_back(q, g).wait_send()

            @pl.when((works == 1) & (z < last_z))
            def _():
                relay(q, g).wait_send()

            keep_copy(q, g).wait()

            @pl.when(r > 0)
            def _():
                pass_copy(q, g).wait_recv()

    @pl.when(r == 0)
    def _():
        first = out.at[0, :, pl.ds(0, rows)]
        pltpu.make_async_copy(first, first, cleared.at[0]).wait()


def shards(inputs, norm_gain, qkv_weight, batch_lengths, doc_lengths, doc_shift):
    chunks, rows, width = inputs.shape
    groups = KVHEADS
    there = pl.BlockSpec(memory_space=pl.ANY)
    dma = pltpu.SemaphoreType.DMA
    state = pltpu.VMEM((chunks, groups, rows, WIDE), BF)
    flags = pltpu.VMEM((chunks, rows, HEAD), F32)
    ring = dma((2, 2 * groups, 2))
    piece, tasks = dma((chunks, groups)), dma((2 * chunks, groups))
    return pl.pallas_call(
        kernel,
        out_shape=jax.ShapeDtypeStruct((1, chunks, 2 * rows, width), BF),
        in_specs=[there] * 6,
        out_specs=there,
        scratch_shapes=[
            pltpu.VMEM((2,) + norm_gain.shape, F32),
            pltpu.VMEM(doc_lengths.shape, jnp.int32),
            pltpu.VMEM(doc_shift.shape, jnp.int32),
            pltpu.SMEM(batch_lengths.shape, jnp.int32),
            dma((groups + 4,)),
            pltpu.VMEM((2 * groups, NY, NX, 2, 2, 32, COLS), BF),
            state,
            pltpu.VMEM((chunks, rows, width), BF),
            state,
            state,
            state,
            pltpu.VMEM((2 * chunks, groups, rows, 2 * HEAD), BF),
            pltpu.VMEM((2 * chunks, groups, 1, rows, 2 * HEAD), BF),
            pltpu.VMEM((groups, rows, WIDE), BF),
            pltpu.VMEM((chunks, 2, rows // 2, rows + rows // 2), F32),
            flags,
            flags,
            flags,
            pltpu.VMEM((rows, WIDE), BF),
            ring, ring, ring, ring, ring, ring, ring, ring,
            dma((2, 2 * groups, 4)), dma((2, 2 * groups, 4)),
            tasks, tasks, piece, piece, piece, piece, piece, piece,
            dma((4,)), dma((4,)), dma((1,)),
        ],
        compiler_params=pltpu.CompilerParams(
            collective_id=0, has_side_effects=True, vmem_limit_bytes=48 << 20
        ),
        name="relay",
    )(inputs, norm_gain, qkv_weight, doc_lengths, doc_shift, batch_lengths)


def solution(mesh):
    placed = (P(None, "cp", None), P("section", None), P("section", "cp", None), P(), P(), P())
    return jax.shard_map(
        shards,
        mesh=mesh,
        in_specs=placed,
        out_specs=P("section", None, "cp", None),
        check_vma=False,
    )
```
